512 devices in a mesh: seq: 64 (over x, z_lo, core), mp: 8 (over z_hi, y).
Axes of the slice: x: 4, y: 4, z: 16 (z_hi: 2, z_lo: 8; z = z_hi * 8 + z_lo), core: 2. Of those that a mesh axis runs over, the one named last changes fastest.
Arguments:
- tokens: bfloat16 [8192, 4096], P('seq', 'mp'), may hold values from -700 to 700
- norm_gain: float32 [4096], replicated, may hold values from 0.1 to 1.9
- w_qkv: bfloat16 [3, 4096, 4096], P(None, 'seq', 'mp'), may hold values from -0.09375 to 0.09375
- conv_filter: float32 [256, 128], P('mp'), may hold values from -4 to 4
- w_out: bfloat16 [4096, 4096], P('mp'), may hold values from -0.125 to 0.125
Outputs:
- mixed: bfloat16 [8192, 4096], P('seq', 'mp')
The draws below stay inside these ranges and needn't reach their ends.
All inputs are finite; a program needn't handle non-finite values.
Results may differ from the reference program's by a relative error of at most 0.015.
Values may be sent and summed in bfloat16 or wider, within the bound.
A program may use at most 128 MiB of HBM per device.

```python
import math
import jax
import jax.numpy as jnp
from jax import lax

D = 4096
CH = 4096
GROUP_CH = 16
TAPS = 128
GROUPS = 256
TOKENS = 8192
N_MP = 8


def draw_tokens(key, part):
    key = jax.random.fold_in(key, 11)
    key_base, key_rows, key_cols, key_region = jax.random.split(key, 4)
    noise = jnp.clip(jax.random.normal(key_base, (TOKENS, D), jnp.float32), -6.0, 6.0)
    col_scale = jnp.exp(jax.random.uniform(key_cols, (D,), jnp.float32, 0.0, math.log(10.0)))
    row_scale = jnp.exp(jax.random.uniform(key_rows, (TOKENS, 1), jnp.float32, 0.0, math.log(10.0)))
    region = jnp.exp(0.7 * jnp.clip(jax.random.normal(key_region, (8,), jnp.float32), -2.0, 2.0))
    region_of = region[jnp.arange(D) * 8 // D]
    return (noise * row_scale * col_scale * region_of * 0.25).astype(jnp.bfloat16)


def draw_conv_filter(key, part):
    key = jax.random.fold_in(key, 23)
    key_life, key_noise = jax.random.split(key, 2)
    lifetime = jnp.exp(jax.random.uniform(key_life, (GROUPS, 1), jnp.float32, math.log(20.0), math.log(400.0)))
    noise = jnp.clip(jax.random.normal(key_noise, (GROUPS, TAPS), jnp.float32), -4.0, 4.0)
    positions = jnp.arange(TAPS).astype(jnp.float32)[None, :]
    envelope = jnp.exp(-positions / lifetime)
    energy = (1.0 - jnp.exp(-2.0 * TAPS / lifetime)) / (1.0 - jnp.exp(-2.0 / lifetime))
    return (noise * envelope / jnp.sqrt(energy)).astype(jnp.float32)


def strengthened(result, key, source, target, blocks, factor):
    owner, partner = [(jnp.arange(result.shape[axis_at]) // (result.shape[axis_at] // blocks)).reshape([-1 if axis == axis_at else 1 for axis in range(result.ndim)]) for axis_at in (source, target)]
    chosen = jax.random.permutation(key, blocks)[partner]
    strong = (owner == chosen) | (owner == (partner + blocks // 2) % blocks)
    return jnp.where(strong, factor * result, result)


def block_scale(stream_key, extent, shards, least, top_value):
    factor_of = 1.0
    for position, parts in shards:
        draws = jax.random.uniform(jax.random.fold_in(jax.random.fold_in(stream_key, 6), position), (parts,), jnp.float32, least / len(shards), top_value / len(shards))
        factor_of = factor_of * jnp.repeat(jnp.exp(draws), extent[position] // parts).reshape((-1,) + (1,) * (len(extent) - 1 - position))
    return factor_of


def gaussian(stream_key, dims, spread, reach, shards=(), dtype=jnp.bfloat16):
    values = jax.random.normal(stream_key, dims, jnp.float32) * spread
    if len(shards) > 0:
        values = block_scale(stream_key, dims, shards, -0.22, 0.18) * values
    return jnp.clip(values, min=-reach, max=reach).astype(dtype)


def noise_with(rng, shape, spread, limit, cuts, heavy, kind=jnp.bfloat16):
    array = spread * jax.random.normal(rng, shape, jnp.float32)
    if cuts:
        array = array * block_scale(rng, shape, cuts, -0.22, 0.18)
    return jnp.clip(strengthened(array, jax.random.fold_in(rng, 3), *heavy), -limit, limit).astype(kind)


def setup_inputs(seed: int = 0) -> dict:
    streams_of = jax.random.split(jax.random.key(seed), 6)
    tokens = draw_tokens(jax.random.fold_in(streams_of[5], 71), 0)
    norm_gain = jnp.clip(1.0 + 0.18 * jax.random.normal(streams_of[1], (D,), jnp.float32), 0.1, 1.9)
    w_qkv = gaussian(streams_of[2], (3, D, CH), D ** -0.5, 0.09375, ((1, 64), (2, 8)))
    conv_filter = draw_conv_filter(jax.random.fold_in(streams_of[5], 71), 0)
    w_out = noise_with(streams_of[4], (CH, D), CH ** -0.5, 0.125, ((0, 8),), (0, 1, 8, 2.0))
    return {"tokens": tokens, "norm_gain": norm_gain, "w_qkv": w_qkv, "conv_filter": conv_filter, "w_out": w_out}


def reference(tokens, norm_gain, w_qkv, conv_filter, w_out):
    tokens_f = tokens.astype(jnp.float32)
    factor = lax.rsqrt(lax.optimization_barrier(jnp.mean(tokens_f * tokens_f, axis=1, keepdims=True)) + 1e-05)
    normed = (tokens_f * factor * norm_gain).astype(jnp.bfloat16)
    queries = jnp.dot(normed, w_qkv[0], preferred_element_type=jnp.float32).astype(jnp.bfloat16)
    key_proj = jnp.dot(normed, w_qkv[1], preferred_element_type=jnp.float32).astype(jnp.bfloat16)
    values_proj = jnp.dot(normed, w_qkv[2], preferred_element_type=jnp.float32).astype(jnp.bfloat16)
    kv_prod = (key_proj.astype(jnp.float32) * values_proj.astype(jnp.float32)).astype(jnp.bfloat16)
    per_channel = jnp.repeat(conv_filter, GROUP_CH, axis=0)
    padded = jnp.concatenate([jnp.zeros((TAPS - 1, CH), jnp.float32), kv_prod.astype(jnp.float32)], axis=0)

    def add_tap(tap_index, running):
        tap_int = jnp.asarray(tap_index).astype(jnp.int32)
        offset = (TAPS - 1 - tap_int).astype(jnp.int32)
        shifted = lax.dynamic_slice_in_dim(padded, offset, TOKENS, 0)
        weight = lax.dynamic_slice_in_dim(per_channel, tap_int, 1, 1)[:, 0]
        return running + weight * shifted
    convolved = lax.fori_loop(0, TAPS, add_tap, jnp.zeros((TOKENS, CH), jnp.float32))
    gated_out = (queries.astype(jnp.float32) * convolved).astype(jnp.bfloat16)
    share_width = CH // N_MP

    def add_share(share_index, running):
        offset = (jnp.asarray(share_index).astype(jnp.int32) * share_width).astype(jnp.int32)
        part_in = lax.dynamic_slice_in_dim(gated_out, offset, share_width, 1)
        part_w = lax.dynamic_slice_in_dim(w_out, offset, share_width, 0)
        partial_value = jnp.dot(part_in, part_w, preferred_element_type=jnp.float32).astype(jnp.bfloat16)
        partial_value = lax.optimization_barrier(partial_value)
        return running + partial_value.astype(jnp.float32)
    summed = lax.fori_loop(0, N_MP, add_share, jnp.zeros((TOKENS, D), jnp.float32))
    return summed.astype(jnp.bfloat16)
```

```python
import functools

import jax
import jax.numpy as jnp
from jax import lax
from jax.experimental import pallas as pl
from jax.experimental.pallas import tpu as pltpu
from jax.sharding import PartitionSpec as P

NX, NZ, NY = 4, 8, 4
TAPS = 128
LAG_X, LAG_H = 3, 4
F32, BF16 = jnp.float32, jnp.bfloat16


def dot(a, b):
    return jnp.dot(a, b, preferred_element_type=F32)


def kernel(
    tok_in, gain, w_in, filt, wout_in, out,
    wbuf, tok, normed, acc, kvb, halo, frev, tcur, tprev, wout, part, peers, zsum, zpeer,
    loc, z_s, z_r, x_s, x_r, h_s, h_r, d_s, d_r, tz_s, tz_r, ty_s, ty_r, hl_s, hl_r, rs_s, rs_r, rz_s, rz_r,
):
    seq, mp = lax.axis_index("seq"), lax.axis_index("mp")
    core, p, x = seq % 2, (seq // 2) % NZ, seq // (2 * NZ)
    zhi, y = mp // NY, mp % NY
    rows = tok_in.shape[0]
    depth = w_in.shape[1]
    width = w_in.shape[2]
    column = 2 * NZ * depth
    sibling = (seq + 1 - 2 * core, mp)
    across = (seq, (mp + NY) % (2 * NY))
    n_seq = 2 * NZ * NX

    def along_x(d):
        return ((seq + (2 * NZ if d == 0 else n_seq - 2 * NZ)) % n_seq, mp)

    def along_z(d):
        return (seq + (2 if d == 0 else -2), mp)

    def along_y(o):
        return (seq, zhi * NY + (y + o) % NY)

    def remote(src, dst, s, r, dev):
        return pltpu.make_async_remote_copy(
            src_ref=src, dst_ref=dst, send_sem=s, recv_sem=r,
            device_id=dev, device_id_type=pl.DeviceIdType.MESH,
        )

    own_w = pl.ds(pl.multiple_of(seq * depth, depth), depth)
    load_tok = pltpu.make_async_copy(tok_in, tok.at[mp], loc.at[0])
    load_w = pltpu.make_async_copy(w_in, wbuf.at[:, own_w, :], loc.at[1])
    load_wout = pltpu.make_async_copy(wout_in, wout, loc.at[2])
    load_tok.start()
    load_w.start()
    load_wout.start()

    barrier = pltpu.get_barrier_semaphore()

    def greet(dev):
        pl.semaphore_signal(barrier, inc=1, device_id=dev, device_id_type=pl.DeviceIdType.MESH)

    for dev in (along_x(0), along_x(1), sibling, across, along_y(1), along_y(2), along_y(3)):
        greet(dev)
    has_up, has_down = p < NZ - 1, p > 0
    has_far = jnp.where(core == 0, seq > 0, seq < n_seq - 1)
    far = jnp.where(core == 0, seq - 1, seq + 1)

    @pl.when(has_up)
    def _():
        greet(along_z(0))

    @pl.when(has_down)
    def _():
        greet(along_z(1))

    @pl.when(has_far)
    def _():
        greet((far, mp))

    load_tok.wait()
    load_w.wait()
    pl.semaphore_wait(
        barrier, 7 + has_up.astype(jnp.int32) + has_down.astype(jnp.int32) + has_far.astype(jnp.int32)
    )

    tok_z = remote(tok.at[mp], tok.at[mp], tz_s.at[0], tz_r.at[0], across)
    tok_z.start()

    def tok_y(half, o):
        m = mp if half == 0 else (mp + NY) % (2 * NY)
        return remote(tok.at[m], tok.at[m], ty_s.at[half, o - 1], ty_r.at[half, o - 1], along_y(o))

    def tok_y_arrival(half, o):
        m = (zhi if half == 0 else 1 - zhi) * NY + (y + NY - o) % NY
        return remote(tok.at[m], tok.at[m], ty_s.at[half, o - 1], ty_r.at[half, o - 1], along_y(o))

    for o in (2, 1, 3):
        tok_y(0, o).start()

    def block(xx, j, c):
        return wbuf.at[:, pl.ds(pl.multiple_of(((xx * NZ + j) * 2 + c) * depth, depth), depth), :]

    def half_block(xx, j, c, h):
        at = ((xx * NZ + j) * 2 + c) * depth + h * (depth // 2)
        return wbuf.at[:, pl.ds(pl.multiple_of(at, depth // 2), depth // 2), :]

    def z_copy(d, j):
        return remote(block(x, j, core), block(x, j, core), z_s.at[d, j], z_r.at[j], along_z(d))

    def x_copy(d, xx, j):
        return remote(block(xx, j, core), block(xx, j, core), x_s.at[d, j], x_r.at[d, j], along_x(d))

    def h_copy(d, xx, j):
        ref = half_block(xx, j, core, d)
        return remote(ref, ref, h_s.at[d, j], h_r.at[d, j], along_x(d))

    def d_copy(k, j, c):
        ref = block((x + k) % NX, j, c)
        return remote(ref, ref, d_s.at[k, j], d_r.at[k, j], sibling)

    fewer = jnp.minimum(p, NZ - 1 - p)

    def nth(n):
        paired = jnp.where(n % 2 == 1, p - (n + 1) // 2, p + (n + 1) // 2)
        rest = jnp.where(2 * p < NZ, p + n - fewer, p - n + fewer)
        return jnp.where(n <= 2 * fewer, paired, rest)

    def stage_z(n):
        j = nth(n)

        @pl.when(n > 0)
        def _():
            z_copy(0, j).wait_recv()

        @pl.when(has_up & (j <= p))
        def _():
            z_copy(0, j).start()

        @pl.when(has_down & (j >= p))
        def _():
            z_copy(1, j).start()

        x_copy(0, x, j).start()
        x_copy(1, x, j).start()
        d_copy(0, j, core).start()

    def stage_x(n):
        j = nth(n)
        left, right = (x + NX - 1) % NX, (x + 1) % NX
        x_copy(0, left, j).wait_recv()
        h_copy(0, left, j).start()
        d_copy(3, j, core).start()
        x_copy(1, right, j).wait_recv()
        h_copy(1, right, j).start()
        d_copy(1, j, core).start()

    def stage_h(n):
        j = nth(n)
        opposite = (x + 2) % NX
        h_copy(0, opposite, j).wait_recv()
        h_copy(1, opposite, j).wait_recv()
        d_copy(2, j, core).start()

    def steps(first, last):
        def step(n, carry):
            @pl.when(n < NZ)
            def _():
                stage_z(n)

            @pl.when((n >= LAG_X) & (n < NZ + LAG_X))
            def _():
                stage_x(n - LAG_X)

            @pl.when(n >= LAG_H)
            def _():
                stage_h(n - LAG_H)

            return carry

        lax.fori_loop(first, last, step, 0)

    def from_sibling(k):
        def one(j, carry):
            d_copy(k, j, 1 - core).wait_recv()
            return carry

        lax.fori_loop(0, NZ, one, 0)

    steps(0, 1)

    lane = lax.broadcasted_iota(jnp.int32, (TAPS, TAPS), 1)
    row = lax.broadcasted_iota(jnp.int32, (TAPS, TAPS), 0)
    flip = jnp.where(lane + row == TAPS - 1, 1.0, 0.0).astype(BF16)
    frev[...] = dot(filt[...].astype(BF16), flip)

    def build(g, carry):
        spread = jnp.broadcast_to(frev[pl.ds(g, 1), :], (TAPS, TAPS))
        turned = pltpu.roll(spread, 1, 1, stride=1, stride_axis=0)
        tcur[g] = jnp.where(lane <= row, turned, 0.0).astype(BF16)
        tprev[g] = jnp.where(lane > row, turned, 0.0).astype(BF16)
        return carry

    lax.fori_loop(0, filt.shape[0], build, 0)

    steps(1, 3)
    tok_z.wait_recv()
    for o in (2, 1, 3):
        tok_y(1, o).start()
    steps(3, 6)

    for half in range(2):
        for o in (1, 2, 3):
            tok_y_arrival(half, o).wait_recv()
    squares = jnp.zeros((rows, 128), F32)
    for m in range(2 * NY):
        for c in range(width // 128):
            v = tok[m, :, c * 128 : (c + 1) * 128].astype(F32)
            squares = squares + v * v
    factor = lax.rsqrt(jnp.sum(squares, axis=1, keepdims=True) / (2 * NY * width) + 1e-05)
    per = column // width
    for m in range(2 * NY):
        v = tok[m].astype(F32) * factor * gain[:, m * width : (m + 1) * width]
        normed[m // per, :, (m % per) * width : (m % per + 1) * width] = v.astype(BF16)

    def weights(i, xx):
        return wbuf[i, pl.ds(pl.multiple_of(xx * column, column), column), :]

    def multiply(k):
        xx = (x + k) % NX
        for i in range(2):
            product = dot(normed[xx], weights(1 + i, xx))
            if k == 0:
                acc[i] = product
            else:
                acc[i] += product

    steps(6, NZ)
    from_sibling(0)
    multiply(0)
    steps(NZ, NZ + LAG_X)
    from_sibling(3)
    multiply(3)
    from_sibling(1)
    multiply(1)
    steps(NZ + LAG_X, NZ + LAG_H)
    from_sibling(2)
    multiply(2)

    key, value = acc[0].astype(BF16).astype(F32), acc[1].astype(BF16).astype(F32)
    kvb[...] = (key * value).astype(BF16)
    hand_on = remote(kvb, halo, hl_s.at[0], hl_r.at[0], ((seq + 1) % n_seq, mp))

    @pl.when(seq < n_seq - 1)
    def _():
        hand_on.start()

    @pl.when(seq == 0)
    def _():
        halo[...] = jnp.zeros_like(halo)

    q = dot(normed[0], weights(0, 0))
    for xx in range(1, NX):
        q = q + dot(normed[xx], weights(0, xx))
    acc[0] = q.astype(BF16).astype(F32)

    groups = filt.shape[0]
    of_lane = lane // (width // groups)
    per_tile = 128 // (width // groups)

    def convolve(mats, source, t):
        lhs = mats[t * per_tile : (t + 1) * per_tile].reshape(per_tile * TAPS, TAPS)
        wide = dot(lhs, source[:, t * 128 : (t + 1) * 128])
        total = jnp.zeros((TAPS, 128), F32)
        for g in range(per_tile):
            total = jnp.where(of_lane == g, wide[g * TAPS : (g + 1) * TAPS], total)
        return total

    for t in range(width // 128):
        acc[1, :, t * 128 : (t + 1) * 128] = convolve(tcur, kvb, t)

    @pl.when(seq > 0)
    def _():
        hand_on.wait_recv()

    for t in range(width // 128):
        at = slice(t * 128, (t + 1) * 128)
        convolved = acc[1, :, at] + convolve(tprev, halo, t)
        normed[0, :, at] = (acc[0, :, at] * convolved).astype(BF16)

    load_wout.wait()
    gated = normed[0, :, :width]

    def share(m):
        return dot(gated, wout[:, pl.ds(pl.multiple_of(m * width, width), width)])

    def exchange(o, zsel):
        m = (zhi if zsel == 1 else 1 - zhi) * NY + (y + o) % NY
        return remote(part.at[o - 1, zsel], peers.at[o - 1, zsel], rs_s.at[o - 1, zsel], rs_r.at[o - 1, zsel], along_y(o)), m

    for zsel in range(2):
        for o in (2, 1, 3):
            copy, m = exchange(o, zsel)
            part[o - 1, zsel] = share(m).astype(BF16)
            copy.start()
    acc[0] = share((1 - zhi) * NY + y).astype(BF16).astype(F32)
    for o in (1, 3, 2):
        exchange(o, 0)[0].wait_recv()
    zsum[...] = (acc[0] + peers[0, 0].astype(F32) + peers[1, 0].astype(F32) + peers[2, 0].astype(F32)).astype(BF16)
    cross = remote(zsum, zpeer, rz_s.at[0], rz_r.at[0], across)
    cross.start()
    acc[1] = share(mp).astype(BF16).astype(F32)
    for o in (1, 3, 2):
        exchange(o, 1)[0].wait_recv()
    acc[1] = acc[1] + peers[0, 1].astype(F32) + peers[1, 1].astype(F32) + peers[2, 1].astype(F32)

    def sent(j, carry):
        @pl.when(has_up & (j <= p))
        def _():
            z_copy(0, j).wait_send()

        @pl.when(has_down & (j >= p))
        def _():
            z_copy(1, j).wait_send()

        for d in range(2):
            x_copy(d, x, j).wait_send()
            h_copy(d, x, j).wait_send()
        for k in range(NX):
            d_copy(k, j, core).wait_send()
        return carry

    lax.fori_loop(0, NZ, sent, 0)
    tok_z.wait_send()
    for half in range(2):
        for o in (1, 2, 3):
            tok_y(half, o).wait_send()
    for zsel in range(2):
        for o in (1, 2, 3):
            exchange(o, zsel)[0].wait_send()

    @pl.when(seq < n_seq - 1)
    def _():
        hand_on.wait_send()

    cross.wait()
    out[...] = (acc[1] + zpeer[...].astype(F32)).astype(BF16)


def local(tokens, norm_gain, w_qkv, conv_filter, w_out):
    rows, width = tokens.shape
    features = norm_gain.shape[0]
    depth = w_qkv.shape[1]
    groups = conv_filter.shape[0]
    dma = pltpu.SemaphoreType.DMA
    column = 2 * NZ * depth
    scratch = [
        pltpu.VMEM((3, features, width), BF16),
        pltpu.VMEM((2 * NY, rows, width), BF16),
        pltpu.VMEM((NX, rows, column), BF16),
        pltpu.VMEM((2, rows, width), F32),
        pltpu.VMEM((rows, width), BF16),
        pltpu.VMEM((rows, width), BF16),
        pltpu.VMEM((groups, TAPS), F32),
        pltpu.VMEM((groups, TAPS, TAPS), BF16),
        pltpu.VMEM((groups, TAPS, TAPS), BF16),
        pltpu.VMEM(w_out.shape, BF16),
        pltpu.VMEM((NY - 1, 2, rows, width), BF16),
        pltpu.VMEM((NY - 1, 2, rows, width), BF16),
        pltpu.VMEM((rows, width), BF16),
        pltpu.VMEM((rows, width), BF16),
    ]
    sems = [(3,), (2, NZ), (NZ,), (2, NZ), (2, NZ), (2, NZ), (2, NZ), (NX, NZ), (NX, NZ)]
    sems += [(1,), (1,), (2, NY - 1), (2, NY - 1), (1,), (1,), (NY - 1, 2), (NY - 1, 2), (1,), (1,)]
    hbm, vmem = pl.BlockSpec(memory_space=pl.ANY), pl.BlockSpec(memory_space=pltpu.VMEM)
    return pl.pallas_call(
        kernel,
        out_shape=jax.ShapeDtypeStruct((rows, width), BF16),
        in_specs=[hbm, vmem, hbm, vmem, hbm],
        out_specs=vmem,
        scratch_shapes=scratch + [dma(s) for s in sems],
        compiler_params=pltpu.CompilerParams(
            collective_id=0, has_side_effects=True, vmem_limit_bytes=50 * 1024 * 1024
        ),
        cost_estimate=pl.CostEstimate(flops=2300000000, bytes_accessed=20000000, transcendentals=0),
    )(tokens, norm_gain.reshape(1, features), w_qkv, conv_filter, w_out)


def solution(mesh):
    placed = (P("seq", "mp"), P(), P(None, "seq", "mp"), P("mp", None), P("mp", None))
    return jax.shard_map(
        local, mesh=mesh, in_specs=placed, out_specs=P("seq", "mp"), check_vma=False
    )
```

```python
import functools

import jax
import jax.numpy as jnp
from jax import lax
from jax.experimental import pallas as pl
from jax.experimental.pallas import tpu as pltpu
from jax.sharding import PartitionSpec as P

NX, NZ, NY = 4, 8, 4
TAPS = 128
SPLIT = 2
F32, BF16 = jnp.float32, jnp.bfloat16


def dot(a, b):
    return jnp.dot(a, b, preferred_element_type=F32)


def kernel(
    tok_in, gain_in, w_in, filt_in, wout_in, out,
    wbuf, tok, normed, acc, kvb, halo, gain, filt, frev, tcur, tprev, wout, part, peers, zsum, zpeer,
    loc, z_s, z_r, x_s, x_r, d_s, d_r, own_r, tz_s, tz_r, ty_s, ty_r, hl_s, hl_r, rs_s, rs_r, rz_s, rz_r,
):
    seq, mp = lax.axis_index("seq"), lax.axis_index("mp")
    core, p, x = seq % 2, (seq // 2) % NZ, seq // (2 * NZ)
    zhi, y = mp // NY, mp % NY
    rows = tok_in.shape[0]
    depth = w_in.shape[1]
    width = w_in.shape[2]
    chunk = 2 * depth
    column = NZ * chunk
    cut = width // SPLIT
    sibling = (seq + 1 - 2 * core, mp)
    across = (seq, (mp + NY) % (2 * NY))
    n_seq = 2 * NZ * NX

    def along_x(k):
        return ((seq + 2 * NZ * k) % n_seq, mp)

    def along_z(d):
        return (seq + (2 if d == 0 else -2), mp)

    def along_y(o):
        return (seq, zhi * NY + (y + o) % NY)

    def remote(src, dst, s, r, dev):
        return pltpu.make_async_remote_copy(
            src_ref=src, dst_ref=dst, send_sem=s, recv_sem=r,
            device_id=dev, device_id_type=pl.DeviceIdType.MESH,
        )

    own_w = pl.ds(pl.multiple_of(seq * depth, depth), depth)
    loads = [
        pltpu.make_async_copy(filt_in, filt, loc.at[0]),
        pltpu.make_async_copy(tok_in, tok.at[mp], loc.at[1]),
        pltpu.make_async_copy(w_in, wbuf.at[:, own_w, :], loc.at[2]),
        pltpu.make_async_copy(gain_in, gain, loc.at[3]),
        pltpu.make_async_copy(wout_in, wout, loc.at[4]),
    ]
    for load in loads:
        load.start()

    barrier = pltpu.get_barrier_semaphore()

    def greet(dev):
        pl.semaphore_signal(barrier, inc=1, device_id=dev, device_id_type=pl.DeviceIdType.MESH)

    for dev in [sibling, across] + [along_x(k) for k in (1, 2, 3)] + [along_y(o) for o in (1, 2, 3)]:
        greet(dev)
    has_up, has_down = p < NZ - 1, p > 0
    has_far = jnp.where(core == 0, seq > 0, seq < n_seq - 1)
    far = jnp.where(core == 0, seq - 1, seq + 1)

    @pl.when(has_up)
    def _():
        greet(along_z(0))

    @pl.when(has_down)
    def _():
        greet(along_z(1))

    @pl.when(has_far)
    def _():
        greet((far, mp))

    lane = lax.broadcasted_iota(jnp.int32, (TAPS, TAPS), 1)
    row = lax.broadcasted_iota(jnp.int32, (TAPS, TAPS), 0)
    flip = jnp.where(lane + row == TAPS - 1, 1.0, 0.0).astype(BF16)
    loads[0].wait()
    frev[...] = dot(filt[...].astype(BF16), flip)

    def build(g, carry):
        spread = jnp.broadcast_to(frev[pl.ds(g, 1), :], (TAPS, TAPS))
        turned = pltpu.roll(spread, 1, 1, stride=1, stride_axis=0)
        tcur[g] = jnp.where(lane <= row, turned, 0.0).astype(BF16)
        tprev[g] = jnp.where(lane > row, turned, 0.0).astype(BF16)
        return carry

    lax.fori_loop(0, filt.shape[0], build, 0)
    for load in loads[1:4]:
        load.wait()
    pl.semaphore_wait(
        barrier, 8 + has_up.astype(jnp.int32) + has_down.astype(jnp.int32) + has_far.astype(jnp.int32)
    )

    tok_z = remote(tok.at[mp], tok.at[mp], tz_s.at[0], tz_r.at[0], across)
    tok_z.start()

    def tok_y(half, o):
        m = mp if half == 0 else (mp + NY) % (2 * NY)
        return remote(tok.at[m], tok.at[m], ty_s.at[half, o - 1], ty_r.at[half, o - 1], along_y(o))

    def tok_y_arrival(half, o):
        m = (zhi if half == 0 else 1 - zhi) * NY + (y + NY - o) % NY
        return remote(tok.at[m], tok.at[m], ty_s.at[half, o - 1], ty_r.at[half, o - 1], along_y(o))

    for o in (2, 1, 3):
        tok_y(0, o).start()

    def rows_of(piece, start, count):
        which = pl.ds(1, 2) if piece == 0 else pl.ds(0, 1)
        return wbuf.at[which, pl.ds(pl.multiple_of(start, depth), count), :]

    def block(piece, xx, j, c):
        return rows_of(piece, ((xx * NZ + j) * 2 + c) * depth, depth)

    def z_copy(piece, d, j):
        ref = block(piece, x, j, core)
        return remote(ref, ref, z_s.at[piece, d, j], z_r.at[piece, j], along_z(d))

    def x_copy(piece, k, xx, j):
        ref = block(piece, xx, j, core)
        return remote(ref, ref, x_s.at[piece, k - 1], x_r.at[piece, k - 1, j], along_x(k))

    def d_copy(piece, k, j, c):
        ref = block(piece, (x + k) % NX, j, c)
        arrived = own_r.at[piece] if k == 0 else d_r.at[piece, k - 1, j]
        return remote(ref, ref, d_s.at[piece], arrived, sibling)

    fewer = jnp.minimum(p, NZ - 1 - p)

    def nth(n):
        paired = jnp.where(n % 2 == 1, p - (n + 1) // 2, p + (n + 1) // 2)
        rest = jnp.where(2 * p < NZ, p + n - fewer, p - n + fewer)
        return jnp.where(n <= 2 * fewer, paired, rest)

    def stage_z(piece, n):
        j = nth(n)

        @pl.when(n > 0)
        def _():
            z_copy(piece, 0, j).wait_recv()

        @pl.when(has_up & (j <= p))
        def _():
            z_copy(piece, 0, j).start()

        @pl.when(has_down & (j >= p))
        def _():
            z_copy(piece, 1, j).start()

        for k in (2, 1, 3):
            x_copy(piece, k, x, j).start()
        d_copy(piece, 0, j, core).start()

    def stage_x(piece, n):
        j = nth(n)
        for k in (1, 3, 2):
            x_copy(piece, k, (x + NX - k) % NX, j).wait_recv()
            d_copy(piece, NX - k, j, core).start()

    def loop(first, last, *stages):
        def step(n, carry):
            for stage in stages:
                stage(n)
            return carry

        lax.fori_loop(first, last, step, 0)

    loop(0, 4, functools.partial(stage_z, 0))
    tok_z.wait_recv()
    for o in (2, 1, 3):
        tok_y(1, o).start()
    loop(4, NZ, functools.partial(stage_z, 0))

    for half in range(2):
        for o in (1, 2, 3):
            tok_y_arrival(half, o).wait_recv()
    squares = jnp.zeros((rows, 128), F32)
    for m in range(2 * NY):
        for c in range(width // 128):
            v = tok[m, :, c * 128 : (c + 1) * 128].astype(F32)
            squares = squares + v * v
    factor = lax.rsqrt(jnp.sum(squares, axis=1, keepdims=True) / (2 * NY * width) + 1e-05)
    per = column // width
    for m in range(2 * NY):
        v = tok[m].astype(F32) * factor * gain[:, m * width : (m + 1) * width]
        normed[m // per, :, (m % per) * width : (m % per + 1) * width] = v.astype(BF16)

    def multiply_own(piece):
        whole = rows_of(piece, x * column, NZ * depth)
        remote(whole, whole, d_s.at[piece], own_r.at[piece], sibling).wait_recv()
        at = pl.ds(pl.multiple_of(x * column, column), column)
        for i in (1, 2) if piece == 0 else (0,):
            acc[i] = dot(normed[x], wbuf[i, at, :])

    def multiply(piece, n):
        j = nth(n)
        lhs, at = [], []
        for k in (1, 2, 3):
            d_copy(piece, k, j, 1 - core).wait_recv()
            xx = (x + k) % NX
            lhs.append(normed[xx, :, pl.ds(pl.multiple_of(j * chunk, chunk), chunk)])
            at.append(pl.ds(pl.multiple_of((xx * NZ + j) * chunk, chunk), chunk))
        lhs = jnp.concatenate(lhs, axis=1)
        for i in (1, 2) if piece == 0 else (0,):
            acc[i] += dot(lhs, jnp.concatenate([wbuf[i, a, :] for a in at], axis=0))

    def late(piece):
        def stage(n):
            @pl.when(n > 0)
            def _():
                multiply(piece, n - 1)

        return stage

    multiply_own(0)
    loop(0, NZ, functools.partial(stage_x, 0), functools.partial(stage_z, 1), late(0))
    multiply(0, NZ - 1)

    key, value = acc[1].astype(BF16).astype(F32), acc[2].astype(BF16).astype(F32)
    kvb[...] = (key * value).astype(BF16)
    hand_on = remote(kvb, halo, hl_s.at[0], hl_r.at[0], ((seq + 1) % n_seq, mp))

    @pl.when(seq < n_seq - 1)
    def _():
        hand_on.start()

    @pl.when(seq == 0)
    def _():
        halo[...] = jnp.zeros_like(halo)

    groups = filt.shape[0]
    of_lane = lane // (width // groups)
    per_tile = 128 // (width // groups)

    def convolve(mats, source, t):
        lhs = mats[t * per_tile : (t + 1) * per_tile].reshape(per_tile * TAPS, TAPS)
        wide = dot(lhs, source[:, t * 128 : (t + 1) * 128])
        total = jnp.zeros((TAPS, 128), F32)
        for g in range(per_tile):
            total = jnp.where(of_lane == g, wide[g * TAPS : (g + 1) * TAPS], total)
        return total

    for t in range(width // 128):
        acc[1, :, t * 128 : (t + 1) * 128] = convolve(tcur, kvb, t)
    multiply_own(1)
    loop(0, 4, functools.partial(stage_x, 1), late(1))

    @pl.when(seq > 0)
    def _():
        hand_on.wait_recv()

    for t in range(width // 128):
        acc[1, :, t * 128 : (t + 1) * 128] += convolve(tprev, halo, t)
    loads[4].wait()
    loop(4, NZ, functools.partial(stage_x, 1), late(1))
    multiply(1, NZ - 1)
    gated = (acc[0].astype(BF16).astype(F32) * acc[1]).astype(BF16)
    normed[0, :, :width] = gated

    def share(m, c):
        return dot(normed[0, :, :width], wout[:, pl.ds(pl.multiple_of(m * width + c * cut, cut), cut)])

    def exchange(o, zsel, c):
        ref = (o - 1, zsel * SPLIT + c)
        return remote(part.at[ref], peers.at[ref], rs_s.at[ref], rs_r.at[ref], along_y(o))

    def cross(c):
        return remote(zsum.at[c], zpeer.at[c], rz_s.at[c], rz_r.at[c], across)

    for zsel in range(2):
        target = (zhi if zsel == 1 else 1 - zhi) * NY
        for c in range(SPLIT):
            for o in (2, 1, 3):
                part[o - 1, zsel * SPLIT + c] = share(target + (y + o) % NY, c).astype(BF16)
                exchange(o, zsel, c).start()
            acc[zsel, :, c * cut : (c + 1) * cut] = share(target + y, c).astype(BF16).astype(F32)
    for zsel in range(2):
        for c in range(SPLIT):
            total = acc[zsel, :, c * cut : (c + 1) * cut]
            for o in (1, 3, 2):
                exchange(o, zsel, c).wait_recv()
            for o in (1, 2, 3):
                total = total + peers[o - 1, zsel * SPLIT + c].astype(F32)
            if zsel == 0:
                zsum[c] = total.astype(BF16)
                cross(c).start()
            else:
                acc[1, :, c * cut : (c + 1) * cut] = total

    def sent(j, carry):
        for piece in range(2):
            @pl.when(has_up & (j <= p))
            def _():
                z_copy(piece, 0, j).wait_send()

            @pl.when(has_down & (j >= p))
            def _():
                z_copy(piece, 1, j).wait_send()

        return carry

    lax.fori_loop(0, NZ, sent, 0)
    for piece in range(2):
        eight, all_own = rows_of(piece, 0, NZ * depth), rows_of(piece, 0, NX * NZ * depth)
        for k in (1, 2, 3):
            remote(eight, eight, x_s.at[piece, k - 1], x_r.at[piece, k - 1, 0], along_x(k)).wait_send()
        remote(all_own, all_own, d_s.at[piece], own_r.at[piece], sibling).wait_send()
    tok_z.wait_send()
    for half in range(2):
        for o in (1, 2, 3):
            tok_y(half, o).wait_send()
    for zsel in range(2):
        for c in range(SPLIT):
            for o in (1, 2, 3):
                exchange(o, zsel, c).wait_send()

    @pl.when(seq < n_seq - 1)
    def _():
        hand_on.wait_send()

    for c in range(SPLIT):
        cross(c).wait()
        out[:, c * cut : (c + 1) * cut] = (acc[1, :, c * cut : (c + 1) * cut] + zpeer[c].astype(F32)).astype(BF16)


def local(tokens, norm_gain, w_qkv, conv_filter, w_out):
    rows, width = tokens.shape
    features = norm_gain.shape[0]
    depth = w_qkv.shape[1]
    groups = conv_filter.shape[0]
    dma = pltpu.SemaphoreType.DMA
    column = 2 * NZ * depth
    cut = width // SPLIT
    scratch = [
        pltpu.VMEM((3, features, width), BF16),
        pltpu.VMEM((2 * NY, rows, width), BF16),
        pltpu.VMEM((NX, rows, column), BF16),
        pltpu.VMEM((3, rows, width), F32),
        pltpu.VMEM((rows, width), BF16),
        pltpu.VMEM((rows, width), BF16),
        pltpu.VMEM((1, features), F32),
        pltpu.VMEM((groups, TAPS), F32),
        pltpu.VMEM((groups, TAPS), F32),
        pltpu.VMEM((groups, TAPS, TAPS), BF16),
        pltpu.VMEM((groups, TAPS, TAPS), BF16),
        pltpu.VMEM(w_out.shape, BF16),
        pltpu.VMEM((NY - 1, 2 * SPLIT, rows, cut), BF16),
        pltpu.VMEM((NY - 1, 2 * SPLIT, rows, cut), BF16),
        pltpu.VMEM((SPLIT, rows, cut), BF16),
        pltpu.VMEM((SPLIT, rows, cut), BF16),
    ]
    sems = [(5,), (2, 2, NZ), (2, NZ), (2, NX - 1), (2, NX - 1, NZ), (2,), (2, NX - 1, NZ), (2,)]
    sems += [(1,), (1,), (2, NY - 1), (2, NY - 1), (1,), (1,)]
    sems += [(NY - 1, 2 * SPLIT), (NY - 1, 2 * SPLIT), (SPLIT,), (SPLIT,)]
    hbm, vmem = pl.BlockSpec(memory_space=pl.ANY), pl.BlockSpec(memory_space=pltpu.VMEM)
    return pl.pallas_call(
        kernel,
        out_shape=jax.ShapeDtypeStruct((rows, width), BF16),
        in_specs=[hbm] * 5,
        out_specs=vmem,
        scratch_shapes=scratch + [dma(s) for s in sems],
        compiler_params=pltpu.CompilerParams(
            collective_id=0, has_side_effects=True, vmem_limit_bytes=60 * 1024 * 1024
        ),
        cost_estimate=pl.CostEstimate(flops=2300000000, bytes_accessed=20000000, transcendentals=0),
    )(tokens, norm_gain.reshape(1, features), w_qkv, conv_filter, w_out)


def solution(mesh):
    placed = (P("seq", "mp"), P(), P(None, "seq", "mp"), P("mp", None), P("mp", None))
    return jax.shard_map(
        local, mesh=mesh, in_specs=placed, out_specs=P("seq", "mp"), check_vma=False
    )
```

```python
import jax
import jax.numpy as jnp
from jax import lax
from jax.experimental import pallas as pl
from jax.experimental.pallas import tpu as pltpu
from jax.sharding import PartitionSpec as P

NX, NZ, NY = 4, 8, 4
TAPS = 128
TOKENS_AT = 3
SPLIT = 2
F32, BF16 = jnp.float32, jnp.bfloat16


def dot(a, b):
    return jnp.dot(a, b, preferred_element_type=F32)


def kernel(
    tok_in, gain_in, w_in, filt_in, wout_in, out,
    wbuf, tok, gath, scaled, acc, sends, arrivals, kvb, halo, gated, gain, filt, frev, tcur, tprev, wout,
    part, peers, zsum, zpeer,
    loc, z_s, z_r, d_s, d_r, tx_s, tx_r, q_s, q_r, tz_s, tz_r, ty_s, ty_r, hl_s, hl_r, rs_s, rs_r, rz_s, rz_r,
):
    seq, mp = lax.axis_index("seq"), lax.axis_index("mp")
    core, p, x = seq % 2, (seq // 2) % NZ, seq // (2 * NZ)
    zhi, y = mp // NY, mp % NY
    rows = tok_in.shape[0]
    depth = w_in.shape[1]
    width = w_in.shape[2]
    chunk = 2 * depth
    column = NZ * chunk
    cut = width // SPLIT
    sibling = (seq + 1 - 2 * core, mp)
    across = (seq, (mp + NY) % (2 * NY))
    n_seq = 2 * NZ * NX

    def along_x(k):
        return ((seq + 2 * NZ * k) % n_seq, mp)

    def along_z(d):
        return (seq + (2 if d == 0 else -2), mp)

    def along_y(o):
        return (seq, zhi * NY + (y + o) % NY)

    def remote(src, dst, s, r, dev):
        return pltpu.make_async_remote_copy(
            src_ref=src, dst_ref=dst, send_sem=s, recv_sem=r,
            device_id=dev, device_id_type=pl.DeviceIdType.MESH,
        )

    own_w = pl.ds(pl.multiple_of((2 * p + core) * depth, depth), depth)
    loads = [
        pltpu.make_async_copy(filt_in, filt, loc.at[0]),
        pltpu.make_async_copy(tok_in, tok.at[mp], loc.at[1]),
        pltpu.make_async_copy(w_in, wbuf.at[:, own_w, :], loc.at[2]),
        pltpu.make_async_copy(gain_in, gain, loc.at[3]),
        pltpu.make_async_copy(wout_in, wout, loc.at[4]),
    ]
    for load in loads:
        load.start()

    barrier = pltpu.get_barrier_semaphore()

    def greet(dev):
        pl.semaphore_signal(barrier, inc=1, device_id=dev, device_id_type=pl.DeviceIdType.MESH)

    for dev in [sibling, across] + [along_x(k) for k in (1, 2, 3)] + [along_y(o) for o in (1, 2, 3)]:
        greet(dev)
    has_up, has_down = p < NZ - 1, p > 0
    has_far = jnp.where(core == 0, seq > 0, seq < n_seq - 1)
    far = jnp.where(core == 0, seq - 1, seq + 1)

    @pl.when(has_up)
    def _():
        greet(along_z(0))

    @pl.when(has_down)
    def _():
        greet(along_z(1))

    @pl.when(has_far)
    def _():
        greet((far, mp))

    lane = lax.broadcasted_iota(jnp.int32, (TAPS, TAPS), 1)
    row = lax.broadcasted_iota(jnp.int32, (TAPS, TAPS), 0)
    flip = jnp.where(lane + row == TAPS - 1, 1.0, 0.0).astype(BF16)
    loads[0].wait()
    frev[...] = dot(filt[...].astype(BF16), flip)

    def build(g, carry):
        spread = jnp.broadcast_to(frev[pl.ds(g, 1), :], (TAPS, TAPS))
        turned = pltpu.roll(spread, 1, 1, stride=1, stride_axis=0)
        tcur[g] = jnp.where(lane <= row, turned, 0.0).astype(BF16)
        tprev[g] = jnp.where(lane > row, turned, 0.0).astype(BF16)
        return carry

    lax.fori_loop(0, filt.shape[0], build, 0)
    for load in loads[1:4]:
        load.wait()
    pl.semaphore_wait(
        barrier, 8 + has_up.astype(jnp.int32) + has_down.astype(jnp.int32) + has_far.astype(jnp.int32)
    )

    tok_z = remote(tok.at[mp], tok.at[mp], tz_s.at[0], tz_r.at[0], across)
    tok_z.start()

    def tok_y(half, o):
        m = mp if half == 0 else (mp + NY) % (2 * NY)
        return remote(tok.at[m], tok.at[m], ty_s.at[half, o - 1], ty_r.at[half, o - 1], along_y(o))

    def tok_y_arrival(half, o):
        m = (zhi if half == 0 else 1 - zhi) * NY + (y + NY - o) % NY
        return remote(tok.at[m], tok.at[m], ty_s.at[half, o - 1], ty_r.at[half, o - 1], along_y(o))

    for o in (2, 1, 3):
        tok_y(0, o).start()

    def tok_x(k):
        to = (x + k) % NX
        return remote(tok.at[pl.ds(2 * to, 2)], gath.at[k - 1], tx_s.at[k - 1], tx_r.at[k - 1], along_x(k))

    def tok_x_start(half):
        for k in (2, 1, 3):
            here = ((x + k) % NX) // 2 == zhi

            @pl.when(here if half == 0 else jnp.logical_not(here))
            def _():
                tok_x(k).start()

    def rows_of(piece, start, count):
        which = pl.ds(1, 2) if piece == 0 else pl.ds(0, 1)
        return wbuf.at[which, pl.ds(pl.multiple_of(start, depth), count), :]

    def block(piece, j, c):
        return rows_of(piece, (j * 2 + c) * depth, depth)

    def z_copy(piece, d, j):
        ref = block(piece, j, core)
        return remote(ref, ref, z_s.at[piece, d, j], z_r.at[piece, j], along_z(d))

    def d_copy(piece, j, c):
        ref = block(piece, j, c)
        return remote(ref, ref, d_s.at[piece], d_r.at[piece, j], sibling)

    fewer = jnp.minimum(p, NZ - 1 - p)

    def nth(n):
        paired = jnp.where(n % 2 == 1, p - (n + 1) // 2, p + (n + 1) // 2)
        rest = jnp.where(2 * p < NZ, p + n - fewer, p - n + fewer)
        return jnp.where(n <= 2 * fewer, paired, rest)

    def pass_on(piece, j, first):
        if not first:
            z_copy(piece, 0, j).wait_recv()

        @pl.when(has_up & (j <= p))
        def _():
            z_copy(piece, 0, j).start()

        @pl.when(has_down & (j >= p))
        def _():
            z_copy(piece, 1, j).start()

        d_copy(piece, j, core).start()

    def stage_z(piece, k):
        @pl.when(k == 0)
        def _():
            pass_on(piece, p, True)

        @pl.when((k > 0) & (p - k >= 0))
        def _():
            pass_on(piece, p - k, False)

        @pl.when((k > 0) & (p + k < NZ))
        def _():
            pass_on(piece, p + k, False)

    def loop(first, last, step):
        def one(n, carry):
            step(n)
            return carry

        lax.fori_loop(first, last, one, 0)

    kinds = ((1, 2), (0,))

    def pair(piece, n):
        at, lanes = [], []
        for j in (nth(2 * n), nth(2 * n + 1)):
            d_copy(piece, j, 1 - core).wait_recv()
            at.append(pl.ds(pl.multiple_of(j * chunk, chunk), chunk))
        return at

    def multiply(piece, n):
        at = pair(piece, n)
        lhs = jnp.concatenate([scaled[:, :, a].reshape(NX * rows, chunk) for a in at], axis=1)
        for i in kinds[piece]:
            product = dot(lhs, jnp.concatenate([wbuf[i, a, :] for a in at], axis=0))
            acc[i] += product.reshape(NX, rows, width)

    def send_sum(piece, k):
        which = pl.ds(1, 2) if piece == 0 else pl.ds(0, 1)
        return remote(
            sends.at[k - 1, which], arrivals.at[k - 1, which], q_s.at[piece, k - 1], q_r.at[piece, k - 1], along_x(k)
        )

    def multiply_last(piece, n):
        at = pair(piece, n)
        for k in (2, 1, 3, 0):
            lhs = jnp.concatenate([scaled[k, :, a] for a in at], axis=1)
            for i in kinds[piece]:
                total = acc[i, k] + dot(lhs, jnp.concatenate([wbuf[i, a, :] for a in at], axis=0))
                if k > 0:
                    sends[k - 1, i] = total.astype(BF16)
                else:
                    acc[i, 0] = total
            if k > 0:
                send_sum(piece, k).start()

    def collect_sum(i):
        total = acc[i, 0]
        for k in (1, 2, 3):
            total = total + arrivals[k - 1, i].astype(F32)
        return (total * factor).astype(BF16).astype(F32)

    loop(0, 2, lambda k: stage_z(0, k))
    acc[...] = jnp.zeros_like(acc)
    for o in (1, 3, 2):
        tok_y_arrival(0, o).wait_recv()
    tok_x_start(0)
    loop(2, TOKENS_AT, lambda k: stage_z(0, k))
    tok_z.wait_recv()
    for o in (2, 1, 3):
        tok_y(1, o).start()
    loop(TOKENS_AT, TOKENS_AT + 2, lambda k: stage_z(0, k))
    for o in (1, 3, 2):
        tok_y_arrival(1, o).wait_recv()
    tok_x_start(1)
    loop(TOKENS_AT + 2, NZ, lambda k: stage_z(0, k))
    stage_z(1, 0)

    squares = jnp.zeros((rows, 128), F32)
    for m in range(2 * NY):
        for c in range(width // 128):
            v = tok[m, :, c * 128 : (c + 1) * 128].astype(F32)
            squares = squares + v * v
    factor = lax.rsqrt(jnp.sum(squares, axis=1, keepdims=True) / (2 * NY * width) + 1e-05)
    for h in range(2):
        g = gain[:, pl.ds(pl.multiple_of((2 * x + h) * width, width), width)]
        at = slice(h * width, (h + 1) * width)
        scaled[0, :, at] = (tok[2 * x + h].astype(F32) * g).astype(BF16)
    for k in (1, 3, 2):
        tok_x(k).wait_recv()
        for h in range(2):
            g = gain[:, pl.ds(pl.multiple_of((2 * x + h) * width, width), width)]
            at = slice(h * width, (h + 1) * width)
            scaled[NX - k, :, at] = (gath[k - 1, h].astype(F32) * g).astype(BF16)

    def middle(n):
        multiply(0, n)
        stage_z(1, n + 1)

    loop(0, NZ // 2 - 1, middle)
    multiply_last(0, NZ // 2 - 1)
    loop(NZ // 2, NZ, lambda k: stage_z(1, k))
    loop(0, NZ // 2 - 1, lambda n: multiply(1, n))
    multiply_last(1, NZ // 2 - 1)

    for k in (1, 3, 2):
        send_sum(0, k).wait_recv()
    kvb[...] = (collect_sum(1) * collect_sum(2)).astype(BF16)
    hand_on = remote(kvb, halo, hl_s.at[0], hl_r.at[0], ((seq + 1) % n_seq, mp))

    @pl.when(seq < n_seq - 1)
    def _():
        hand_on.start()

    @pl.when(seq == 0)
    def _():
        halo[...] = jnp.zeros_like(halo)

    groups = filt.shape[0]
    of_lane = lane // (width // groups)
    per_tile = 128 // (width // groups)

    def convolve(mats, source, t):
        lhs = mats[t * per_tile : (t + 1) * per_tile].reshape(per_tile * TAPS, TAPS)
        wide = dot(lhs, source[:, t * 128 : (t + 1) * 128])
        total = jnp.zeros((TAPS, 128), F32)
        for g in range(per_tile):
            total = jnp.where(of_lane == g, wide[g * TAPS : (g + 1) * TAPS], total)
        return total

    for t in range(width // 128):
        acc[1, 0, :, t * 128 : (t + 1) * 128] = convolve(tcur, kvb, t)

    @pl.when(seq > 0)
    def _():
        hand_on.wait_recv()

    for t in range(width // 128):
        acc[1, 0, :, t * 128 : (t + 1) * 128] += convolve(tprev, halo, t)
    loads[4].wait()
    for k in (1, 3, 2):
        send_sum(1, k).wait_recv()
    gated[...] = (collect_sum(0) * acc[1, 0]).astype(BF16)

    def share(m, c):
        return dot(gated[...], wout[:, pl.ds(pl.multiple_of(m * width + c * cut, cut), cut)])

    def exchange(o, zsel, c):
        ref = (o - 1, zsel * SPLIT + c)
        return remote(part.at[ref], peers.at[ref], rs_s.at[ref], rs_r.at[ref], along_y(o))

    def cross(c):
        return remote(zsum.at[c], zpeer.at[c], rz_s.at[c], rz_r.at[c], across)

    def hand_out(zsel, c):
        target = (zhi if zsel == 1 else 1 - zhi) * NY
        for o in (2, 1, 3):
            part[o - 1, zsel * SPLIT + c] = share(target + (y + o) % NY, c).astype(BF16)
            exchange(o, zsel, c).start()

    def keep(zsel, c):
        own = share((zhi if zsel == 1 else 1 - zhi) * NY + y, c)
        acc[1, 1 + zsel, :, c * cut : (c + 1) * cut] = own.astype(BF16).astype(F32)

    def collect(zsel, c):
        total = acc[1, 1 + zsel, :, c * cut : (c + 1) * cut]
        for o in (1, 3, 2):
            exchange(o, zsel, c).wait_recv()
        for o in (1, 2, 3):
            total = total + peers[o - 1, zsel * SPLIT + c].astype(F32)
        return total

    for c in range(SPLIT):
        hand_out(0, c)
    for c in range(SPLIT):
        keep(0, c)
    for c in range(SPLIT):
        zsum[c] = collect(0, c).astype(BF16)
        cross(c).start()
    for c in range(SPLIT):
        hand_out(1, c)
        keep(1, c)
    for c in range(SPLIT):
        acc[1, 2, :, c * cut : (c + 1) * cut] = collect(1, c)

    def sent(j, carry):
        for piece in range(2):
            @pl.when(has_up & (j <= p))
            def _():
                z_copy(piece, 0, j).wait_send()

            @pl.when(has_down & (j >= p))
            def _():
                z_copy(piece, 1, j).wait_send()

        return carry

    lax.fori_loop(0, NZ, sent, 0)
    for piece in range(2):
        eight = rows_of(piece, 0, NZ * depth)
        remote(eight, eight, d_s.at[piece], d_r.at[piece, 0], sibling).wait_send()
        for k in (1, 2, 3):
            send_sum(piece, k).wait_send()
    for k in (1, 2, 3):
        tok_x(k).wait_send()
    tok_z.wait_send()
    for half in range(2):
        for o in (1, 2, 3):
            tok_y(half, o).wait_send()
    for zsel in range(2):
        for c in range(SPLIT):
            for o in (1, 2, 3):
                exchange(o, zsel, c).wait_send()

    @pl.when(seq < n_seq - 1)
    def _():
        hand_on.wait_send()

    for c in range(SPLIT):
        cross(c).wait()
        out[:, c * cut : (c + 1) * cut] = (acc[1, 2, :, c * cut : (c + 1) * cut] + zpeer[c].astype(F32)).astype(BF16)


def local(tokens, norm_gain, w_qkv, conv_filter, w_out):
    rows, width = tokens.shape
    features = norm_gain.shape[0]
    depth = w_qkv.shape[1]
    groups = conv_filter.shape[0]
    dma = pltpu.SemaphoreType.DMA
    column = 2 * NZ * depth
    cut = width // SPLIT
    scratch = [
        pltpu.VMEM((3, column, width), BF16),
        pltpu.VMEM((2 * NY, rows, width), BF16),
        pltpu.VMEM((NX - 1, 2, rows, width), BF16),
        pltpu.VMEM((NX, rows, column), BF16),
        pltpu.VMEM((3, NX, rows, width), F32),
        pltpu.VMEM((NX - 1, 3, rows, width), BF16),
        pltpu.VMEM((NX - 1, 3, rows, width), BF16),
        pltpu.VMEM((rows, width), BF16),
        pltpu.VMEM((rows, width), BF16),
        pltpu.VMEM((rows, width), BF16),
        pltpu.VMEM((1, features), F32),
        pltpu.VMEM((groups, TAPS), F32),
        pltpu.VMEM((groups, TAPS), F32),
        pltpu.VMEM((groups, TAPS, TAPS), BF16),
        pltpu.VMEM((groups, TAPS, TAPS), BF16),
        pltpu.VMEM(w_out.shape, BF16),
        pltpu.VMEM((NY - 1, 2 * SPLIT, rows, cut), BF16),
        pltpu.VMEM((NY - 1, 2 * SPLIT, rows, cut), BF16),
        pltpu.VMEM((SPLIT, rows, cut), BF16),
        pltpu.VMEM((SPLIT, rows, cut), BF16),
    ]
    sems = [(5,), (2, 2, NZ), (2, NZ), (2,), (2, NZ), (NX - 1,), (NX - 1,), (2, NX - 1), (2, NX - 1)]
    sems += [(1,), (1,), (2, NY - 1), (2, NY - 1), (1,), (1,)]
    sems += [(NY - 1, 2 * SPLIT), (NY - 1, 2 * SPLIT), (SPLIT,), (SPLIT,)]
    hbm, vmem = pl.BlockSpec(memory_space=pl.ANY), pl.BlockSpec(memory_space=pltpu.VMEM)
    return pl.pallas_call(
        kernel,
        out_shape=jax.ShapeDtypeStruct((rows, width), BF16),
        in_specs=[hbm] * 5,
        out_specs=vmem,
        scratch_shapes=scratch + [dma(s) for s in sems],
        compiler_params=pltpu.CompilerParams(
            collective_id=0, has_side_effects=True, vmem_limit_bytes=60 * 1024 * 1024
        ),
        cost_estimate=pl.CostEstimate(flops=2300000000, bytes_accessed=20000000, transcendentals=0),
    )(tokens, norm_gain.reshape(1, features), w_qkv, conv_filter, w_out)


def solution(mesh):
    placed = (P("seq", "mp"), P(), P(None, "seq", "mp"), P("mp", None), P("mp", None))
    return jax.shard_map(
        local, mesh=mesh, in_specs=placed, out_specs=P("seq", "mp"), check_vma=False
    )
```

```python
import jax
import jax.numpy as jnp
from jax import lax
from jax.experimental import pallas as pl
from jax.experimental.pallas import tpu as pltpu
from jax.sharding import PartitionSpec as P

NX, NZ, NY = 4, 8, 4
TAPS = 128
LAG = 2
TOKENS_AT = 3
SPLIT = 2
F32, BF16 = jnp.float32, jnp.bfloat16


def dot(a, b):
    return jnp.dot(a, b, preferred_element_type=F32)


def kernel(
    tok_in, gain_in, w_in, filt_in, wout_in, out,
    wbuf, tok, gath, scaled, acc, sends, arrivals, kvb, halo, gated, gain, filt, frev, tcur, tprev, wout,
    part, peers, zsum, zpeer,
    loc, z_s, z_r, d_s, d_r, tx_s, tx_r, q_s, q_r, tz_s, tz_r, ty_s, ty_r, hl_s, hl_r, rs_s, rs_r, rz_s, rz_r,
):
    seq, mp = lax.axis_index("seq"), lax.axis_index("mp")
    core, p, x = seq % 2, (seq // 2) % NZ, seq // (2 * NZ)
    zhi, y = mp // NY, mp % NY
    rows = tok_in.shape[0]
    depth = w_in.shape[1]
    width = w_in.shape[2]
    chunk = 2 * depth
    column = NZ * chunk
    cut = width // SPLIT
    sibling = (seq + 1 - 2 * core, mp)
    across = (seq, (mp + NY) % (2 * NY))
    n_seq = 2 * NZ * NX

    def along_x(k):
        return ((seq + 2 * NZ * k) % n_seq, mp)

    def along_z(d):
        return (seq + (2 if d == 0 else -2), mp)

    def along_y(o):
        return (seq, zhi * NY + (y + o) % NY)

    def remote(src, dst, s, r, dev):
        return pltpu.make_async_remote_copy(
            src_ref=src, dst_ref=dst, send_sem=s, recv_sem=r,
            device_id=dev, device_id_type=pl.DeviceIdType.MESH,
        )

    own_w = pl.ds(pl.multiple_of((2 * p + core) * depth, depth), depth)
    loads = [
        pltpu.make_async_copy(filt_in, filt, loc.at[0]),
        pltpu.make_async_copy(tok_in, tok.at[mp], loc.at[1]),
        pltpu.make_async_copy(w_in, wbuf.at[:, own_w, :], loc.at[2]),
        pltpu.make_async_copy(gain_in, gain, loc.at[3]),
        pltpu.make_async_copy(wout_in, wout, loc.at[4]),
    ]
    for load in loads:
        load.start()

    barrier = pltpu.get_barrier_semaphore()

    def greet(dev):
        pl.semaphore_signal(barrier, inc=1, device_id=dev, device_id_type=pl.DeviceIdType.MESH)

    for dev in [sibling, across] + [along_x(k) for k in (1, 2, 3)] + [along_y(o) for o in (1, 2, 3)]:
        greet(dev)
    has_up, has_down = p < NZ - 1, p > 0
    has_far = jnp.where(core == 0, seq > 0, seq < n_seq - 1)
    far = jnp.where(core == 0, seq - 1, seq + 1)

    @pl.when(has_up)
    def _():
        greet(along_z(0))

    @pl.when(has_down)
    def _():
        greet(along_z(1))

    @pl.when(has_far)
    def _():
        greet((far, mp))

    lane = lax.broadcasted_iota(jnp.int32, (TAPS, TAPS), 1)
    row = lax.broadcasted_iota(jnp.int32, (TAPS, TAPS), 0)
    flip = jnp.where(lane + row == TAPS - 1, 1.0, 0.0).astype(BF16)
    loads[0].wait()
    frev[...] = dot(filt[...].astype(BF16), flip)

    def build(g, carry):
        spread = jnp.broadcast_to(frev[pl.ds(g, 1), :], (TAPS, TAPS))
        turned = pltpu.roll(spread, 1, 1, stride=1, stride_axis=0)
        tcur[g] = jnp.where(lane <= row, turned, 0.0).astype(BF16)
        tprev[g] = jnp.where(lane > row, turned, 0.0).astype(BF16)
        return carry

    lax.fori_loop(0, filt.shape[0], build, 0)
    for load in loads[1:4]:
        load.wait()
    pl.semaphore_wait(
        barrier, 8 + has_up.astype(jnp.int32) + has_down.astype(jnp.int32) + has_far.astype(jnp.int32)
    )

    tok_z = remote(tok.at[mp], tok.at[mp], tz_s.at[0], tz_r.at[0], across)
    tok_z.start()

    def tok_y(half, o):
        m = mp if half == 0 else (mp + NY) % (2 * NY)
        return remote(tok.at[m], tok.at[m], ty_s.at[half, o - 1], ty_r.at[half, o - 1], along_y(o))

    def tok_y_arrival(half, o):
        m = (zhi if half == 0 else 1 - zhi) * NY + (y + NY - o) % NY
        return remote(tok.at[m], tok.at[m], ty_s.at[half, o - 1], ty_r.at[half, o - 1], along_y(o))

    for o in (2, 1, 3):
        tok_y(0, o).start()

    def tok_x(k):
        to = (x + k) % NX
        return remote(tok.at[pl.ds(2 * to, 2)], gath.at[k - 1], tx_s.at[k - 1], tx_r.at[k - 1], along_x(k))

    def tok_x_start(half):
        for k in (2, 1, 3):
            here = ((x + k) % NX) // 2 == zhi

            @pl.when(here if half == 0 else jnp.logical_not(here))
            def _():
                tok_x(k).start()

    def block(i, j, c):
        return wbuf.at[i, pl.ds(pl.multiple_of((j * 2 + c) * depth, depth), depth), :]

    def z_copy(i, d, j):
        ref = block(i, j, core)
        return remote(ref, ref, z_s.at[i, d, j], z_r.at[i, j], along_z(d))

    def d_copy(i, j, c):
        ref = block(i, j, c)
        return remote(ref, ref, d_s.at[i], d_r.at[i, j], sibling)

    fewer = jnp.minimum(p, NZ - 1 - p)

    def nth(n):
        paired = jnp.where(n % 2 == 1, p - (n + 1) // 2, p + (n + 1) // 2)
        rest = jnp.where(2 * p < NZ, p + n - fewer, p - n + fewer)
        return jnp.where(n <= 2 * fewer, paired, rest)

    def pass_on(i, j, first):
        if not first:
            z_copy(i, 0, j).wait_recv()

        @pl.when(has_up & (j <= p))
        def _():
            z_copy(i, 0, j).start()

        @pl.when(has_down & (j >= p))
        def _():
            z_copy(i, 1, j).start()

        d_copy(i, j, core).start()

    def stage_z(i, k):
        @pl.when(k == 0)
        def _():
            pass_on(i, p, True)

        @pl.when((k > 0) & (p - k >= 0))
        def _():
            pass_on(i, p - k, False)

        @pl.when((k > 0) & (p + k < NZ))
        def _():
            pass_on(i, p + k, False)

    def step_z(k):
        stage_z(1, k)
        stage_z(2, k)

        @pl.when(k >= LAG)
        def _():
            stage_z(0, k - LAG)

    def loop(first, last, step):
        def one(n, carry):
            step(n)
            return carry

        lax.fori_loop(first, last, one, 0)

    kinds = ((1, 2), (0,))

    def pair(piece, n):
        at, lanes = [], []
        for j in (nth(2 * n), nth(2 * n + 1)):
            for i in kinds[piece]:
                d_copy(i, j, 1 - core).wait_recv()
            at.append(pl.ds(pl.multiple_of(j * chunk, chunk), chunk))
        return at

    def multiply(piece, n):
        at = pair(piece, n)
        lhs = jnp.concatenate([scaled[:, :, a].reshape(NX * rows, chunk) for a in at], axis=1)
        for i in kinds[piece]:
            product = dot(lhs, jnp.concatenate([wbuf[i, a, :] for a in at], axis=0))
            acc[i] += product.reshape(NX, rows, width)

    def send_sum(piece, k):
        which = pl.ds(1, 2) if piece == 0 else pl.ds(0, 1)
        return remote(
            sends.at[k - 1, which], arrivals.at[k - 1, which], q_s.at[piece, k - 1], q_r.at[piece, k - 1], along_x(k)
        )

    def multiply_last(piece, n):
        at = pair(piece, n)
        for k in (2, 1, 3, 0):
            lhs = jnp.concatenate([scaled[k, :, a] for a in at], axis=1)
            for i in kinds[piece]:
                total = acc[i, k] + dot(lhs, jnp.concatenate([wbuf[i, a, :] for a in at], axis=0))
                if k > 0:
                    sends[k - 1, i] = total.astype(BF16)
                else:
                    acc[i, 0] = total
            if k > 0:
                send_sum(piece, k).start()

    def collect_sum(i):
        total = acc[i, 0]
        for k in (1, 2, 3):
            total = total + arrivals[k - 1, i].astype(F32)
        return (total * factor).astype(BF16).astype(F32)

    loop(0, 2, step_z)
    acc[...] = jnp.zeros_like(acc)
    for o in (1, 3, 2):
        tok_y_arrival(0, o).wait_recv()
    tok_x_start(0)
    loop(2, TOKENS_AT, step_z)
    tok_z.wait_recv()
    for o in (2, 1, 3):
        tok_y(1, o).start()
    loop(TOKENS_AT, TOKENS_AT + 2, step_z)
    for o in (1, 3, 2):
        tok_y_arrival(1, o).wait_recv()
    tok_x_start(1)
    loop(TOKENS_AT + 2, NZ, step_z)

    squares = jnp.zeros((rows, 128), F32)
    for m in range(2 * NY):
        for c in range(width // 128):
            v = tok[m, :, c * 128 : (c + 1) * 128].astype(F32)
            squares = squares + v * v
    factor = lax.rsqrt(jnp.sum(squares, axis=1, keepdims=True) / (2 * NY * width) + 1e-05)
    for h in range(2):
        g = gain[:, pl.ds(pl.multiple_of((2 * x + h) * width, width), width)]
        at = slice(h * width, (h + 1) * width)
        scaled[0, :, at] = (tok[2 * x + h].astype(F32) * g).astype(BF16)
    for k in (1, 3, 2):
        tok_x(k).wait_recv()
        for h in range(2):
            g = gain[:, pl.ds(pl.multiple_of((2 * x + h) * width, width), width)]
            at = slice(h * width, (h + 1) * width)
            scaled[NX - k, :, at] = (gath[k - 1, h].astype(F32) * g).astype(BF16)

    def middle(n):
        multiply(0, n)
        stage_z(0, NZ - LAG + n)

    loop(0, min(LAG, NZ // 2 - 1), middle)
    loop(min(LAG, NZ // 2 - 1), NZ // 2 - 1, lambda n: multiply(0, n))
    multiply_last(0, NZ // 2 - 1)
    loop(NZ - LAG + min(LAG, NZ // 2 - 1), NZ, lambda k: stage_z(0, k))
    loop(0, NZ // 2 - 1, lambda n: multiply(1, n))
    multiply_last(1, NZ // 2 - 1)

    for k in (1, 3, 2):
        send_sum(0, k).wait_recv()
    kvb[...] = (collect_sum(1) * collect_sum(2)).astype(BF16)
    hand_on = remote(kvb, halo, hl_s.at[0], hl_r.at[0], ((seq + 1) % n_seq, mp))

    @pl.when(seq < n_seq - 1)
    def _():
        hand_on.start()

    @pl.when(seq == 0)
    def _():
        halo[...] = jnp.zeros_like(halo)

    groups = filt.shape[0]
    of_lane = lane // (width // groups)
    per_tile = 128 // (width // groups)

    def convolve(mats, source, t):
        lhs = mats[t * per_tile : (t + 1) * per_tile].reshape(per_tile * TAPS, TAPS)
        wide = dot(lhs, source[:, t * 128 : (t + 1) * 128])
        total = jnp.zeros((TAPS, 128), F32)
        for g in range(per_tile):
            total = jnp.where(of_lane == g, wide[g * TAPS : (g + 1) * TAPS], total)
        return total

    for t in range(width // 128):
        acc[1, 0, :, t * 128 : (t + 1) * 128] = convolve(tcur, kvb, t)

    @pl.when(seq > 0)
    def _():
        hand_on.wait_recv()

    for t in range(width // 128):
        acc[1, 0, :, t * 128 : (t + 1) * 128] += convolve(tprev, halo, t)
    loads[4].wait()
    for k in (1, 3, 2):
        send_sum(1, k).wait_recv()
    gated[...] = (collect_sum(0) * acc[1, 0]).astype(BF16)

    def share(m, c):
        return dot(gated[...], wout[:, pl.ds(pl.multiple_of(m * width + c * cut, cut), cut)])

    def exchange(o, zsel, c):
        ref = (o - 1, zsel * SPLIT + c)
        return remote(part.at[ref], peers.at[ref], rs_s.at[ref], rs_r.at[ref], along_y(o))

    def cross(c):
        return remote(zsum.at[c], zpeer.at[c], rz_s.at[c], rz_r.at[c], across)

    def hand_out(zsel, c):
        target = (zhi if zsel == 1 else 1 - zhi) * NY
        for o in (2, 1, 3):
            part[o - 1, zsel * SPLIT + c] = share(target + (y + o) % NY, c).astype(BF16)
            exchange(o, zsel, c).start()

    def keep(zsel, c):
        own = share((zhi if zsel == 1 else 1 - zhi) * NY + y, c)
        acc[1, 1 + zsel, :, c * cut : (c + 1) * cut] = own.astype(BF16).astype(F32)

    def collect(zsel, c):
        total = acc[1, 1 + zsel, :, c * cut : (c + 1) * cut]
        for o in (1, 3, 2):
            exchange(o, zsel, c).wait_recv()
        for o in (1, 2, 3):
            total = total + peers[o - 1, zsel * SPLIT + c].astype(F32)
        return total

    for c in range(SPLIT):
        hand_out(0, c)
    for c in range(SPLIT):
        keep(0, c)
    for c in range(SPLIT):
        zsum[c] = collect(0, c).astype(BF16)
        cross(c).start()
    for c in range(SPLIT):
        hand_out(1, c)
        keep(1, c)
    for c in range(SPLIT):
        acc[1, 2, :, c * cut : (c + 1) * cut] = collect(1, c)

    def sent(j, carry):
        for i in range(3):
            @pl.when(has_up & (j <= p))
            def _():
                z_copy(i, 0, j).wait_send()

            @pl.when(has_down & (j >= p))
            def _():
                z_copy(i, 1, j).wait_send()

        return carry

    lax.fori_loop(0, NZ, sent, 0)
    for i in range(3):
        eight = wbuf.at[i, pl.ds(0, NZ * depth), :]
        remote(eight, eight, d_s.at[i], d_r.at[i, 0], sibling).wait_send()
    for piece in range(2):
        for k in (1, 2, 3):
            send_sum(piece, k).wait_send()
    for k in (1, 2, 3):
        tok_x(k).wait_send()
    tok_z.wait_send()
    for half in range(2):
        for o in (1, 2, 3):
            tok_y(half, o).wait_send()
    for zsel in range(2):
        for c in range(SPLIT):
            for o in (1, 2, 3):
                exchange(o, zsel, c).wait_send()

    @pl.when(seq < n_seq - 1)
    def _():
        hand_on.wait_send()

    for c in range(SPLIT):
        cross(c).wait()
        out[:, c * cut : (c + 1) * cut] = (acc[1, 2, :, c * cut : (c + 1) * cut] + zpeer[c].astype(F32)).astype(BF16)


def local(tokens, norm_gain, w_qkv, conv_filter, w_out):
    rows, width = tokens.shape
    features = norm_gain.shape[0]
    depth = w_qkv.shape[1]
    groups = conv_filter.shape[0]
    dma = pltpu.SemaphoreType.DMA
    column = 2 * NZ * depth
    cut = width // SPLIT
    scratch = [
        pltpu.VMEM((3, column, width), BF16),
        pltpu.VMEM((2 * NY, rows, width), BF16),
        pltpu.VMEM((NX - 1, 2, rows, width), BF16),
        pltpu.VMEM((NX, rows, column), BF16),
        pltpu.VMEM((3, NX, rows, width), F32),
        pltpu.VMEM((NX - 1, 3, rows, width), BF16),
        pltpu.VMEM((NX - 1, 3, rows, width), BF16),
        pltpu.VMEM((rows, width), BF16),
        pltpu.VMEM((rows, width), BF16),
        pltpu.VMEM((rows, width), BF16),
        pltpu.VMEM((1, features), F32),
        pltpu.VMEM((groups, TAPS), F32),
        pltpu.VMEM((groups, TAPS), F32),
        pltpu.VMEM((groups, TAPS, TAPS), BF16),
        pltpu.VMEM((groups, TAPS, TAPS), BF16),
        pltpu.VMEM(w_out.shape, BF16),
        pltpu.VMEM((NY - 1, 2 * SPLIT, rows, cut), BF16),
        pltpu.VMEM((NY - 1, 2 * SPLIT, rows, cut), BF16),
        pltpu.VMEM((SPLIT, rows, cut), BF16),
        pltpu.VMEM((SPLIT, rows, cut), BF16),
    ]
    sems = [(5,), (3, 2, NZ), (3, NZ), (3,), (3, NZ), (NX - 1,), (NX - 1,), (2, NX - 1), (2, NX - 1)]
    sems += [(1,), (1,), (2, NY - 1), (2, NY - 1), (1,), (1,)]
    sems += [(NY - 1, 2 * SPLIT), (NY - 1, 2 * SPLIT), (SPLIT,), (SPLIT,)]
    hbm, vmem = pl.BlockSpec(memory_space=pl.ANY), pl.BlockSpec(memory_space=pltpu.VMEM)
    return pl.pallas_call(
        kernel,
        out_shape=jax.ShapeDtypeStruct((rows, width), BF16),
        in_specs=[hbm] * 5,
        out_specs=vmem,
        scratch_shapes=scratch + [dma(s) for s in sems],
        compiler_params=pltpu.CompilerParams(
            collective_id=0, has_side_effects=True, vmem_limit_bytes=60 * 1024 * 1024
        ),
        cost_estimate=pl.CostEstimate(flops=2300000000, bytes_accessed=20000000, transcendentals=0),
    )(tokens, norm_gain.reshape(1, features), w_qkv, conv_filter, w_out)


def solution(mesh):
    placed = (P("seq", "mp"), P(), P(None, "seq", "mp"), P("mp", None), P("mp", None))
    return jax.shard_map(
        local, mesh=mesh, in_specs=placed, out_specs=P("seq", "mp"), check_vma=False
    )
```

```python
import jax
import jax.numpy as jnp
from jax import lax
from jax.experimental import pallas as pl
from jax.experimental.pallas import tpu as pltpu
from jax.sharding import PartitionSpec as P

NX, NZ, NY = 4, 8, 4
TAPS = 128
LAG = 2
TOKENS_AT = 2
SPLIT = 2
F32, BF16 = jnp.float32, jnp.bfloat16


def dot(a, b):
    return jnp.dot(a, b, preferred_element_type=F32)


def kernel(
    tok_in, gain_in, w_in, filt_in, wout_in, out,
    wbuf, tok, gath, scaled, acc, sends, arrivals, kvb, halo, gated, gain, filt, frev, tcur, tprev, wout,
    part, peers, zsum, zpeer,
    loc, z_s, z_r, d_s, d_r, tx_s, tx_r, q_s, q_r, tz_s, tz_r, ty_s, ty_r, hl_s, hl_r, rs_s, rs_r, rz_s, rz_r,
):
    seq, mp = lax.axis_index("seq"), lax.axis_index("mp")
    core, p, x = seq % 2, (seq // 2) % NZ, seq // (2 * NZ)
    zhi, y = mp // NY, mp % NY
    rows = tok_in.shape[0]
    depth = w_in.shape[1]
    width = w_in.shape[2]
    chunk = 2 * depth
    column = NZ * chunk
    cut = width // SPLIT
    sibling = (seq + 1 - 2 * core, mp)
    across = (seq, (mp + NY) % (2 * NY))
    n_seq = 2 * NZ * NX

    def along_x(k):
        return ((seq + 2 * NZ * k) % n_seq, mp)

    def along_z(d):
        return (seq + (2 if d == 0 else -2), mp)

    def along_y(o):
        return (seq, zhi * NY + (y + o) % NY)

    def remote(src, dst, s, r, dev):
        return pltpu.make_async_remote_copy(
            src_ref=src, dst_ref=dst, send_sem=s, recv_sem=r,
            device_id=dev, device_id_type=pl.DeviceIdType.MESH,
        )

    own_w = pl.ds(pl.multiple_of((2 * p + core) * depth, depth), depth)
    loads = [
        pltpu.make_async_copy(filt_in, filt, loc.at[0]),
        pltpu.make_async_copy(tok_in, tok.at[mp], loc.at[1]),
        pltpu.make_async_copy(w_in, wbuf.at[:, own_w, :], loc.at[2]),
        pltpu.make_async_copy(gain_in, gain, loc.at[3]),
        pltpu.make_async_copy(wout_in, wout, loc.at[4]),
    ]
    for load in loads:
        load.start()

    barrier = pltpu.get_barrier_semaphore()

    def greet(dev):
        pl.semaphore_signal(barrier, inc=1, device_id=dev, device_id_type=pl.DeviceIdType.MESH)

    for dev in [sibling, across] + [along_x(k) for k in (1, 2, 3)] + [along_y(o) for o in (1, 2, 3)]:
        greet(dev)
    has_up, has_down = p < NZ - 1, p > 0
    has_far = jnp.where(core == 0, seq > 0, seq < n_seq - 1)
    far = jnp.where(core == 0, seq - 1, seq + 1)

    @pl.when(has_up)
    def _():
        greet(along_z(0))

    @pl.when(has_down)
    def _():
        greet(along_z(1))

    @pl.when(has_far)
    def _():
        greet((far, mp))

    lane = lax.broadcasted_iota(jnp.int32, (TAPS, TAPS), 1)
    row = lax.broadcasted_iota(jnp.int32, (TAPS, TAPS), 0)
    flip = jnp.where(lane + row == TAPS - 1, 1.0, 0.0).astype(BF16)
    loads[0].wait()
    frev[...] = dot(filt[...].astype(BF16), flip)

    def build(g, carry):
        spread = jnp.broadcast_to(frev[pl.ds(g, 1), :], (TAPS, TAPS))
        turned = pltpu.roll(spread, 1, 1, stride=1, stride_axis=0)
        tcur[g] = jnp.where(lane <= row, turned, 0.0).astype(BF16)
        tprev[g] = jnp.where(lane > row, turned, 0.0).astype(BF16)
        return carry

    lax.fori_loop(0, filt.shape[0], build, 0)
    for load in loads[1:4]:
        load.wait()
    pl.semaphore_wait(
        barrier, 8 + has_up.astype(jnp.int32) + has_down.astype(jnp.int32) + has_far.astype(jnp.int32)
    )

    tok_z = remote(tok.at[mp], tok.at[mp], tz_s.at[0], tz_r.at[0], across)
    tok_z.start()

    def tok_y(half, o):
        m = mp if half == 0 else (mp + NY) % (2 * NY)
        return remote(tok.at[m], tok.at[m], ty_s.at[half, o - 1], ty_r.at[half, o - 1], along_y(o))

    def tok_y_arrival(half, o):
        m = (zhi if half == 0 else 1 - zhi) * NY + (y + NY - o) % NY
        return remote(tok.at[m], tok.at[m], ty_s.at[half, o - 1], ty_r.at[half, o - 1], along_y(o))

    for o in (2, 1, 3):
        tok_y(0, o).start()

    def tok_x(k):
        to = (x + k) % NX
        return remote(tok.at[pl.ds(2 * to, 2)], gath.at[k - 1], tx_s.at[k - 1], tx_r.at[k - 1], along_x(k))

    def tok_x_start(half):
        for k in (2, 1, 3):
            here = ((x + k) % NX) // 2 == zhi

            @pl.when(here if half == 0 else jnp.logical_not(here))
            def _():
                tok_x(k).start()

    def block(i, j, c):
        return wbuf.at[i, pl.ds(pl.multiple_of((j * 2 + c) * depth, depth), depth), :]

    def z_copy(i, d, j):
        ref = block(i, j, core)
        return remote(ref, ref, z_s.at[i, d, j], z_r.at[i, j], along_z(d))

    def d_copy(i, j, c):
        ref = block(i, j, c)
        return remote(ref, ref, d_s.at[i], d_r.at[i, j], sibling)

    fewer = jnp.minimum(p, NZ - 1 - p)

    def nth(n):
        paired = jnp.where(n % 2 == 1, p - (n + 1) // 2, p + (n + 1) // 2)
        rest = jnp.where(2 * p < NZ, p + n - fewer, p - n + fewer)
        return jnp.where(n <= 2 * fewer, paired, rest)

    def pass_on(i, j, first):
        if not first:
            z_copy(i, 0, j).wait_recv()

        @pl.when(has_up & (j <= p))
        def _():
            z_copy(i, 0, j).start()

        @pl.when(has_down & (j >= p))
        def _():
            z_copy(i, 1, j).start()

        d_copy(i, j, core).start()

    def stage_z(i, k):
        @pl.when(k == 0)
        def _():
            pass_on(i, p, True)

        @pl.when((k > 0) & (p - k >= 0))
        def _():
            pass_on(i, p - k, False)

        @pl.when((k > 0) & (p + k < NZ))
        def _():
            pass_on(i, p + k, False)

    def step_z(k):
        stage_z(1, k)
        stage_z(2, k)

        @pl.when(k >= LAG)
        def _():
            stage_z(0, k - LAG)

    def loop(first, last, step):
        def one(n, carry):
            step(n)
            return carry

        lax.fori_loop(first, last, one, 0)

    kinds = ((1, 2), (0,))

    def pair(piece, n):
        at, lanes = [], []
        for j in (nth(2 * n), nth(2 * n + 1)):
            for i in kinds[piece]:
                d_copy(i, j, 1 - core).wait_recv()
            at.append(pl.ds(pl.multiple_of(j * chunk, chunk), chunk))
        return at

    def multiply(piece, n):
        at = pair(piece, n)
        lhs = jnp.concatenate([scaled[:, :, a].reshape(NX * rows, chunk) for a in at], axis=1)
        for i in kinds[piece]:
            product = dot(lhs, jnp.concatenate([wbuf[i, a, :] for a in at], axis=0))
            acc[i] += product.reshape(NX, rows, width)

    def send_sum(piece, k):
        which = pl.ds(1, 2) if piece == 0 else pl.ds(0, 1)
        return remote(
            sends.at[k - 1, which], arrivals.at[k - 1, which], q_s.at[piece, k - 1], q_r.at[piece, k - 1], along_x(k)
        )

    def multiply_last(piece, n):
        at = pair(piece, n)
        for k in (2, 1, 3, 0):
            lhs = jnp.concatenate([scaled[k, :, a] for a in at], axis=1)
            for i in kinds[piece]:
                total = acc[i, k] + dot(lhs, jnp.concatenate([wbuf[i, a, :] for a in at], axis=0))
                if k > 0:
                    sends[k - 1, i] = total.astype(BF16)
                else:
                    acc[i, 0] = total
            if k > 0:
                send_sum(piece, k).start()

    def collect_sum(i):
        total = acc[i, 0]
        for k in (1, 2, 3):
            total = total + arrivals[k - 1, i].astype(F32)
        return (total * factor).astype(BF16).astype(F32)

    loop(0, 2, step_z)
    acc[...] = jnp.zeros_like(acc)
    for o in (1, 3, 2):
        tok_y_arrival(0, o).wait_recv()
    tok_x_start(0)
    loop(2, TOKENS_AT, step_z)
    tok_z.wait_recv()
    for o in (2, 1, 3):
        tok_y(1, o).start()
    loop(TOKENS_AT, TOKENS_AT + 1, step_z)
    for o in (1, 3, 2):
        tok_y_arrival(1, o).wait_recv()
    tok_x_start(1)
    loop(TOKENS_AT + 1, NZ, step_z)

    squares = jnp.zeros((rows, 128), F32)
    for m in range(2 * NY):
        for c in range(width // 128):
            v = tok[m, :, c * 128 : (c + 1) * 128].astype(F32)
            squares = squares + v * v
    factor = lax.rsqrt(jnp.sum(squares, axis=1, keepdims=True) / (2 * NY * width) + 1e-05)
    for h in range(2):
        g = gain[:, pl.ds(pl.multiple_of((2 * x + h) * width, width), width)]
        at = slice(h * width, (h + 1) * width)
        scaled[0, :, at] = (tok[2 * x + h].astype(F32) * g).astype(BF16)
    for k in (1, 3, 2):
        tok_x(k).wait_recv()
        for h in range(2):
            g = gain[:, pl.ds(pl.multiple_of((2 * x + h) * width, width), width)]
            at = slice(h * width, (h + 1) * width)
            scaled[NX - k, :, at] = (gath[k - 1, h].astype(F32) * g).astype(BF16)

    def middle(n):
        multiply(0, n)
        stage_z(0, NZ - LAG + n)

    loop(0, min(LAG, NZ // 2 - 1), middle)
    loop(min(LAG, NZ // 2 - 1), NZ // 2 - 1, lambda n: multiply(0, n))
    multiply_last(0, NZ // 2 - 1)
    loop(NZ - LAG + min(LAG, NZ // 2 - 1), NZ, lambda k: stage_z(0, k))
    loop(0, NZ // 2 - 1, lambda n: multiply(1, n))
    multiply_last(1, NZ // 2 - 1)

    for k in (1, 3, 2):
        send_sum(0, k).wait_recv()
    kvb[...] = (collect_sum(1) * collect_sum(2)).astype(BF16)
    hand_on = remote(kvb, halo, hl_s.at[0], hl_r.at[0], ((seq + 1) % n_seq, mp))

    @pl.when(seq < n_seq - 1)
    def _():
        hand_on.start()

    @pl.when(seq == 0)
    def _():
        halo[...] = jnp.zeros_like(halo)

    groups = filt.shape[0]
    of_lane = lane // (width // groups)
    per_tile = 128 // (width // groups)

    def convolve(mats, source, t):
        lhs = mats[t * per_tile : (t + 1) * per_tile].reshape(per_tile * TAPS, TAPS)
        wide = dot(lhs, source[:, t * 128 : (t + 1) * 128])
        total = jnp.zeros((TAPS, 128), F32)
        for g in range(per_tile):
            total = jnp.where(of_lane == g, wide[g * TAPS : (g + 1) * TAPS], total)
        return total

    for t in range(width // 128):
        acc[1, 0, :, t * 128 : (t + 1) * 128] = convolve(tcur, kvb, t)

    @pl.when(seq > 0)
    def _():
        hand_on.wait_recv()

    for t in range(width // 128):
        acc[1, 0, :, t * 128 : (t + 1) * 128] += convolve(tprev, halo, t)
    loads[4].wait()
    for k in (1, 3, 2):
        send_sum(1, k).wait_recv()
    gated[...] = (collect_sum(0) * acc[1, 0]).astype(BF16)

    def share(m, c):
        return dot(gated[...], wout[:, pl.ds(pl.multiple_of(m * width + c * cut, cut), cut)])

    def exchange(o, zsel, c):
        ref = (o - 1, zsel * SPLIT + c)
        return remote(part.at[ref], peers.at[ref], rs_s.at[ref], rs_r.at[ref], along_y(o))

    def cross(c):
        return remote(zsum.at[c], zpeer.at[c], rz_s.at[c], rz_r.at[c], across)

    def hand_out(zsel, c):
        target = (zhi if zsel == 1 else 1 - zhi) * NY
        for o in (2, 1, 3):
            part[o - 1, zsel * SPLIT + c] = share(target + (y + o) % NY, c).astype(BF16)
            exchange(o, zsel, c).start()

    def keep(zsel, c):
        own = share((zhi if zsel == 1 else 1 - zhi) * NY + y, c)
        acc[1, 1 + zsel, :, c * cut : (c + 1) * cut] = own.astype(BF16).astype(F32)

    def collect(zsel, c):
        total = acc[1, 1 + zsel, :, c * cut : (c + 1) * cut]
        for o in (1, 3, 2):
            exchange(o, zsel, c).wait_recv()
        for o in (1, 2, 3):
            total = total + peers[o - 1, zsel * SPLIT + c].astype(F32)
        return total

    for c in range(SPLIT):
        hand_out(0, c)
    for c in range(SPLIT):
        keep(0, c)
    for c in range(SPLIT):
        zsum[c] = collect(0, c).astype(BF16)
        cross(c).start()
    for c in range(SPLIT):
        hand_out(1, c)
        keep(1, c)
    for c in range(SPLIT):
        acc[1, 2, :, c * cut : (c + 1) * cut] = collect(1, c)

    def sent(j, carry):
        for i in range(3):
            @pl.when(has_up & (j <= p))
            def _():
                z_copy(i, 0, j).wait_send()

            @pl.when(has_down & (j >= p))
            def _():
                z_copy(i, 1, j).wait_send()

        return carry

    lax.fori_loop(0, NZ, sent, 0)
    for i in range(3):
        eight = wbuf.at[i, pl.ds(0, NZ * depth), :]
        remote(eight, eight, d_s.at[i], d_r.at[i, 0], sibling).wait_send()
    for piece in range(2):
        for k in (1, 2, 3):
            send_sum(piece, k).wait_send()
    for k in (1, 2, 3):
        tok_x(k).wait_send()
    tok_z.wait_send()
    for half in range(2):
        for o in (1, 2, 3):
            tok_y(half, o).wait_send()
    for zsel in range(2):
        for c in range(SPLIT):
            for o in (1, 2, 3):
                exchange(o, zsel, c).wait_send()

    @pl.when(seq < n_seq - 1)
    def _():
        hand_on.wait_send()

    for c in range(SPLIT):
        cross(c).wait()
        out[:, c * cut : (c + 1) * cut] = (acc[1, 2, :, c * cut : (c + 1) * cut] + zpeer[c].astype(F32)).astype(BF16)


def local(tokens, norm_gain, w_qkv, conv_filter, w_out):
    rows, width = tokens.shape
    features = norm_gain.shape[0]
    depth = w_qkv.shape[1]
    groups = conv_filter.shape[0]
    dma = pltpu.SemaphoreType.DMA
    column = 2 * NZ * depth
    cut = width // SPLIT
    scratch = [
        pltpu.VMEM((3, column, width), BF16),
        pltpu.VMEM((2 * NY, rows, width), BF16),
        pltpu.VMEM((NX - 1, 2, rows, width), BF16),
        pltpu.VMEM((NX, rows, column), BF16),
        pltpu.VMEM((3, NX, rows, width), F32),
        pltpu.VMEM((NX - 1, 3, rows, width), BF16),
        pltpu.VMEM((NX - 1, 3, rows, width), BF16),
        pltpu.VMEM((rows, width), BF16),
        pltpu.VMEM((rows, width), BF16),
        pltpu.VMEM((rows, width), BF16),
        pltpu.VMEM((1, features), F32),
        pltpu.VMEM((groups, TAPS), F32),
        pltpu.VMEM((groups, TAPS), F32),
        pltpu.VMEM((groups, TAPS, TAPS), BF16),
        pltpu.VMEM((groups, TAPS, TAPS), BF16),
        pltpu.VMEM(w_out.shape, BF16),
        pltpu.VMEM((NY - 1, 2 * SPLIT, rows, cut), BF16),
        pltpu.VMEM((NY - 1, 2 * SPLIT, rows, cut), BF16),
        pltpu.VMEM((SPLIT, rows, cut), BF16),
        pltpu.VMEM((SPLIT, rows, cut), BF16),
    ]
    sems = [(5,), (3, 2, NZ), (3, NZ), (3,), (3, NZ), (NX - 1,), (NX - 1,), (2, NX - 1), (2, NX - 1)]
    sems += [(1,), (1,), (2, NY - 1), (2, NY - 1), (1,), (1,)]
    sems += [(NY - 1, 2 * SPLIT), (NY - 1, 2 * SPLIT), (SPLIT,), (SPLIT,)]
    hbm, vmem = pl.BlockSpec(memory_space=pl.ANY), pl.BlockSpec(memory_space=pltpu.VMEM)
    return pl.pallas_call(
        kernel,
        out_shape=jax.ShapeDtypeStruct((rows, width), BF16),
        in_specs=[hbm] * 5,
        out_specs=vmem,
        scratch_shapes=scratch + [dma(s) for s in sems],
        compiler_params=pltpu.CompilerParams(
            collective_id=0, has_side_effects=True, vmem_limit_bytes=60 * 1024 * 1024
        ),
        cost_estimate=pl.CostEstimate(flops=2300000000, bytes_accessed=20000000, transcendentals=0),
    )(tokens, norm_gain.reshape(1, features), w_qkv, conv_filter, w_out)


def solution(mesh):
    placed = (P("seq", "mp"), P(), P(None, "seq", "mp"), P("mp", None), P("mp", None))
    return jax.shard_map(
        local, mesh=mesh, in_specs=placed, out_specs=P("seq", "mp"), check_vma=False
    )
```

```python
import jax
import jax.numpy as jnp
from jax import lax
from jax.experimental import pallas as pl
from jax.experimental.pallas import tpu as pltpu
from jax.sharding import PartitionSpec as P

NX, NZ, NY = 4, 8, 4
TAPS = 128
LAG = 2
TOKENS_AT, TURN_AT, SCALE_AT = 2, 3, 7
SPLIT = 2
F32, BF16 = jnp.float32, jnp.bfloat16


def dot(a, b):
    return jnp.dot(a, b, preferred_element_type=F32)


def kernel(
    tok_in, gain_in, w_in, filt_in, wout_in, out,
    wbuf, tok, gath, scaled, acc, sends, arrivals, kvb, halo, gated, gain, filt, frev, tcur, tprev, wout,
    part, peers, zsum, zpeer,
    loc, z_s, z_r, d_s, d_r, tx_s, tx_r, q_s, q_r, tz_s, tz_r, ty_s, ty_r, hl_s, hl_r, rs_s, rs_r, rz_s, rz_r,
):
    seq, mp = lax.axis_index("seq"), lax.axis_index("mp")
    core, p, x = seq % 2, (seq // 2) % NZ, seq // (2 * NZ)
    zhi, y = mp // NY, mp % NY
    rows = tok_in.shape[0]
    depth = w_in.shape[1]
    width = w_in.shape[2]
    chunk = 2 * depth
    column = NZ * chunk
    cut = width // SPLIT
    sibling = (seq + 1 - 2 * core, mp)
    across = (seq, (mp + NY) % (2 * NY))
    n_seq = 2 * NZ * NX

    def along_x(k):
        return ((seq + 2 * NZ * k) % n_seq, mp)

    def along_z(d):
        return (seq + (2 if d == 0 else -2), mp)

    def along_y(o):
        return (seq, zhi * NY + (y + o) % NY)

    def remote(src, dst, s, r, dev):
        return pltpu.make_async_remote_copy(
            src_ref=src, dst_ref=dst, send_sem=s, recv_sem=r,
            device_id=dev, device_id_type=pl.DeviceIdType.MESH,
        )

    own_w = pl.ds(pl.multiple_of((2 * p + core) * depth, depth), depth)
    loads = [
        pltpu.make_async_copy(filt_in, filt, loc.at[0]),
        pltpu.make_async_copy(tok_in, tok.at[mp], loc.at[1]),
        pltpu.make_async_copy(w_in, wbuf.at[:, own_w, :], loc.at[2]),
        pltpu.make_async_copy(gain_in, gain, loc.at[3]),
        pltpu.make_async_copy(wout_in, wout, loc.at[4]),
    ]
    for load in loads:
        load.start()

    barrier = pltpu.get_barrier_semaphore()

    def greet(dev):
        pl.semaphore_signal(barrier, inc=1, device_id=dev, device_id_type=pl.DeviceIdType.MESH)

    for dev in [sibling, across] + [along_x(k) for k in (1, 2, 3)] + [along_y(o) for o in (1, 2, 3)]:
        greet(dev)
    has_up, has_down = p < NZ - 1, p > 0
    has_far = jnp.where(core == 0, seq > 0, seq < n_seq - 1)
    far = jnp.where(core == 0, seq - 1, seq + 1)

    @pl.when(has_up)
    def _():
        greet(along_z(0))

    @pl.when(has_down)
    def _():
        greet(along_z(1))

    @pl.when(has_far)
    def _():
        greet((far, mp))

    lane = lax.broadcasted_iota(jnp.int32, (TAPS, TAPS), 1)
    row = lax.broadcasted_iota(jnp.int32, (TAPS, TAPS), 0)
    flip = jnp.where(lane + row == TAPS - 1, 1.0, 0.0).astype(BF16)
    loads[0].wait()
    frev[...] = dot(filt[...].astype(BF16), flip)

    def build(g, carry):
        spread = jnp.broadcast_to(frev[pl.ds(g, 1), :], (TAPS, TAPS))
        turned = pltpu.roll(spread, 1, 1, stride=1, stride_axis=0)
        tcur[g] = jnp.where(lane <= row, turned, 0.0).astype(BF16)
        tprev[g] = jnp.where(lane > row, turned, 0.0).astype(BF16)
        return carry

    lax.fori_loop(0, filt.shape[0], build, 0)
    for load in loads[1:4]:
        load.wait()
    pl.semaphore_wait(
        barrier, 8 + has_up.astype(jnp.int32) + has_down.astype(jnp.int32) + has_far.astype(jnp.int32)
    )

    tok_z = remote(tok.at[mp], tok.at[mp], tz_s.at[0], tz_r.at[0], across)
    tok_z.start()

    def tok_y(half, o):
        m = mp if half == 0 else (mp + NY) % (2 * NY)
        return remote(tok.at[m], tok.at[m], ty_s.at[half, o - 1], ty_r.at[half, o - 1], along_y(o))

    def tok_y_arrival(half, o):
        m = (zhi if half == 0 else 1 - zhi) * NY + (y + NY - o) % NY
        return remote(tok.at[m], tok.at[m], ty_s.at[half, o - 1], ty_r.at[half, o - 1], along_y(o))

    for o in (2, 1, 3):
        tok_y(0, o).start()

    def tok_x(k):
        to = (x + k) % NX
        return remote(tok.at[pl.ds(2 * to, 2)], gath.at[k - 1], tx_s.at[k - 1], tx_r.at[k - 1], along_x(k))

    def tok_x_start(half):
        for k in (2, 1, 3):
            here = ((x + k) % NX) // 2 == zhi

            @pl.when(here if half == 0 else jnp.logical_not(here))
            def _():
                tok_x(k).start()

    def block(i, j, c):
        return wbuf.at[i, pl.ds(pl.multiple_of((j * 2 + c) * depth, depth), depth), :]

    def z_copy(i, d, j):
        ref = block(i, j, core)
        return remote(ref, ref, z_s.at[i, d, j], z_r.at[i, j], along_z(d))

    def d_copy(i, j, c):
        ref = block(i, j, c)
        return remote(ref, ref, d_s.at[i], d_r.at[i, j], sibling)

    fewer = jnp.minimum(p, NZ - 1 - p)

    def nth(n):
        paired = jnp.where(n % 2 == 1, p - (n + 1) // 2, p + (n + 1) // 2)
        rest = jnp.where(2 * p < NZ, p + n - fewer, p - n + fewer)
        return jnp.where(n <= 2 * fewer, paired, rest)

    def pass_on(i, j, first):
        if not first:
            z_copy(i, 0, j).wait_recv()

        @pl.when(has_up & (j <= p))
        def _():
            z_copy(i, 0, j).start()

        @pl.when(has_down & (j >= p))
        def _():
            z_copy(i, 1, j).start()

        d_copy(i, j, core).start()

    def stage_z(i, k):
        @pl.when(k == 0)
        def _():
            pass_on(i, p, True)

        @pl.when((k > 0) & (p - k >= 0))
        def _():
            pass_on(i, p - k, False)

        @pl.when((k > 0) & (p + k < NZ))
        def _():
            pass_on(i, p + k, False)

    def step_z(k):
        stage_z(1, k)
        stage_z(2, k)

        @pl.when(k >= LAG)
        def _():
            stage_z(0, k - LAG)

    def loop(first, last, step):
        def one(n, carry):
            step(n)
            return carry

        lax.fori_loop(first, last, one, 0)

    kinds = ((1, 2), (0,))

    def pair(piece, n):
        at, lanes = [], []
        for j in (nth(2 * n), nth(2 * n + 1)):
            for i in kinds[piece]:
                d_copy(i, j, 1 - core).wait_recv()
            at.append(pl.ds(pl.multiple_of(j * chunk, chunk), chunk))
        return at

    def multiply(piece, n):
        at = pair(piece, n)
        lhs = jnp.concatenate([scaled[:, :, a].reshape(NX * rows, chunk) for a in at], axis=1)
        for i in kinds[piece]:
            product = dot(lhs, jnp.concatenate([wbuf[i, a, :] for a in at], axis=0))
            acc[i] += product.reshape(NX, rows, width)

    def send_sum(piece, k):
        which = pl.ds(1, 2) if piece == 0 else pl.ds(0, 1)
        return remote(
            sends.at[k - 1, which], arrivals.at[k - 1, which], q_s.at[piece, k - 1], q_r.at[piece, k - 1], along_x(k)
        )

    def multiply_last(piece, n):
        at = pair(piece, n)
        for k in (2, 1, 3, 0):
            lhs = jnp.concatenate([scaled[k, :, a] for a in at], axis=1)
            for i in kinds[piece]:
                total = acc[i, k] + dot(lhs, jnp.concatenate([wbuf[i, a, :] for a in at], axis=0))
                if k > 0:
                    sends[k - 1, i] = total.astype(BF16)
                else:
                    acc[i, 0] = total
            if k > 0:
                send_sum(piece, k).start()

    def collect_sum(i):
        total = acc[i, 0]
        for k in (1, 2, 3):
            total = total + arrivals[k - 1, i].astype(F32)
        return (total * factor).astype(BF16).astype(F32)

    loop(0, 1, step_z)
    acc[...] = jnp.zeros_like(acc)
    for o in (1, 3, 2):
        tok_y_arrival(0, o).wait_recv()
    tok_x_start(0)
    loop(1, TOKENS_AT, step_z)
    tok_z.wait_recv()
    for o in (2, 1, 3):
        tok_y(1, o).start()
    loop(TOKENS_AT, TURN_AT, step_z)
    for o in (1, 3, 2):
        tok_y_arrival(1, o).wait_recv()
    tok_x_start(1)
    loop(TURN_AT, SCALE_AT, step_z)

    squares = jnp.zeros((rows, 128), F32)
    for m in range(2 * NY):
        for c in range(width // 128):
            v = tok[m, :, c * 128 : (c + 1) * 128].astype(F32)
            squares = squares + v * v
    factor = lax.rsqrt(jnp.sum(squares, axis=1, keepdims=True) / (2 * NY * width) + 1e-05)
    for h in range(2):
        g = gain[:, pl.ds(pl.multiple_of((2 * x + h) * width, width), width)]
        at = slice(h * width, (h + 1) * width)
        scaled[0, :, at] = (tok[2 * x + h].astype(F32) * g).astype(BF16)
    for k in (1, 3, 2):
        tok_x(k).wait_recv()
        for h in range(2):
            g = gain[:, pl.ds(pl.multiple_of((2 * x + h) * width, width), width)]
            at = slice(h * width, (h + 1) * width)
            scaled[NX - k, :, at] = (gath[k - 1, h].astype(F32) * g).astype(BF16)

    loop(0, (SCALE_AT - 2) // 2, lambda n: multiply(0, n))
    loop(SCALE_AT, NZ - 1, step_z)
    loop((SCALE_AT - 2) // 2, NZ // 2 - 1, lambda n: multiply(0, n))
    loop(NZ - 1, NZ, step_z)
    multiply_last(0, NZ // 2 - 1)
    loop(NZ - LAG, NZ - 1, lambda k: stage_z(0, k))
    loop(0, NZ // 2 - 1, lambda n: multiply(1, n))
    stage_z(0, NZ - 1)
    multiply_last(1, NZ // 2 - 1)

    for k in (1, 3, 2):
        send_sum(0, k).wait_recv()
    kvb[...] = (collect_sum(1) * collect_sum(2)).astype(BF16)
    hand_on = remote(kvb, halo, hl_s.at[0], hl_r.at[0], ((seq + 1) % n_seq, mp))

    @pl.when(seq < n_seq - 1)
    def _():
        hand_on.start()

    @pl.when(seq == 0)
    def _():
        halo[...] = jnp.zeros_like(halo)

    groups = filt.shape[0]
    of_lane = lane // (width // groups)
    per_tile = 128 // (width // groups)

    def convolve(mats, source, t):
        lhs = mats[t * per_tile : (t + 1) * per_tile].reshape(per_tile * TAPS, TAPS)
        wide = dot(lhs, source[:, t * 128 : (t + 1) * 128])
        total = jnp.zeros((TAPS, 128), F32)
        for g in range(per_tile):
            total = jnp.where(of_lane == g, wide[g * TAPS : (g + 1) * TAPS], total)
        return total

    for t in range(width // 128):
        acc[1, 0, :, t * 128 : (t + 1) * 128] = convolve(tcur, kvb, t)

    @pl.when(seq > 0)
    def _():
        hand_on.wait_recv()

    for t in range(width // 128):
        acc[1, 0, :, t * 128 : (t + 1) * 128] += convolve(tprev, halo, t)
    loads[4].wait()
    for k in (1, 3, 2):
        send_sum(1, k).wait_recv()
    gated[...] = (collect_sum(0) * acc[1, 0]).astype(BF16)

    def share(m, c):
        return dot(gated[...], wout[:, pl.ds(pl.multiple_of(m * width + c * cut, cut), cut)])

    def exchange(o, zsel, c):
        ref = (o - 1, zsel * SPLIT + c)
        return remote(part.at[ref], peers.at[ref], rs_s.at[ref], rs_r.at[ref], along_y(o))

    def cross(c):
        return remote(zsum.at[c], zpeer.at[c], rz_s.at[c], rz_r.at[c], across)

    def hand_out(zsel, c):
        target = (zhi if zsel == 1 else 1 - zhi) * NY
        for o in (2, 1, 3):
            part[o - 1, zsel * SPLIT + c] = share(target + (y + o) % NY, c).astype(BF16)
            exchange(o, zsel, c).start()

    def keep(zsel, c):
        own = share((zhi if zsel == 1 else 1 - zhi) * NY + y, c)
        acc[1, 1 + zsel, :, c * cut : (c + 1) * cut] = own.astype(BF16).astype(F32)

    def collect(zsel, c):
        total = acc[1, 1 + zsel, :, c * cut : (c + 1) * cut]
        for o in (1, 3, 2):
            exchange(o, zsel, c).wait_recv()
        for o in (1, 2, 3):
            total = total + peers[o - 1, zsel * SPLIT + c].astype(F32)
        return total

    for c in range(SPLIT):
        hand_out(0, c)
    for c in range(SPLIT):
        keep(0, c)
    for c in range(SPLIT):
        zsum[c] = collect(0, c).astype(BF16)
        cross(c).start()
    for c in range(SPLIT):
        hand_out(1, c)
        keep(1, c)
    for c in range(SPLIT):
        acc[1, 2, :, c * cut : (c + 1) * cut] = collect(1, c)

    def sent(j, carry):
        for i in range(3):
            @pl.when(has_up & (j <= p))
            def _():
                z_copy(i, 0, j).wait_send()

            @pl.when(has_down & (j >= p))
            def _():
                z_copy(i, 1, j).wait_send()

        return carry

    lax.fori_loop(0, NZ, sent, 0)
    for i in range(3):
        eight = wbuf.at[i, pl.ds(0, NZ * depth), :]
        remote(eight, eight, d_s.at[i], d_r.at[i, 0], sibling).wait_send()
    for piece in range(2):
        for k in (1, 2, 3):
            send_sum(piece, k).wait_send()
    for k in (1, 2, 3):
        tok_x(k).wait_send()
    tok_z.wait_send()
    for half in range(2):
        for o in (1, 2, 3):
            tok_y(half, o).wait_send()
    for zsel in range(2):
        for c in range(SPLIT):
            for o in (1, 2, 3):
                exchange(o, zsel, c).wait_send()

    @pl.when(seq < n_seq - 1)
    def _():
        hand_on.wait_send()

    for c in range(SPLIT):
        cross(c).wait()
        out[:, c * cut : (c + 1) * cut] = (acc[1, 2, :, c * cut : (c + 1) * cut] + zpeer[c].astype(F32)).astype(BF16)


def local(tokens, norm_gain, w_qkv, conv_filter, w_out):
    rows, width = tokens.shape
    features = norm_gain.shape[0]
    depth = w_qkv.shape[1]
    groups = conv_filter.shape[0]
    dma = pltpu.SemaphoreType.DMA
    column = 2 * NZ * depth
    cut = width // SPLIT
    scratch = [
        pltpu.VMEM((3, column, width), BF16),
        pltpu.VMEM((2 * NY, rows, width), BF16),
        pltpu.VMEM((NX - 1, 2, rows, width), BF16),
        pltpu.VMEM((NX, rows, column), BF16),
        pltpu.VMEM((3, NX, rows, width), F32),
        pltpu.VMEM((NX - 1, 3, rows, width), BF16),
        pltpu.VMEM((NX - 1, 3, rows, width), BF16),
        pltpu.VMEM((rows, width), BF16),
        pltpu.VMEM((rows, width), BF16),
        pltpu.VMEM((rows, width), BF16),
        pltpu.VMEM((1, features), F32),
        pltpu.VMEM((groups, TAPS), F32),
        pltpu.VMEM((groups, TAPS), F32),
        pltpu.VMEM((groups, TAPS, TAPS), BF16),
        pltpu.VMEM((groups, TAPS, TAPS), BF16),
        pltpu.VMEM(w_out.shape, BF16),
        pltpu.VMEM((NY - 1, 2 * SPLIT, rows, cut), BF16),
        pltpu.VMEM((NY - 1, 2 * SPLIT, rows, cut), BF16),
        pltpu.VMEM((SPLIT, rows, cut), BF16),
        pltpu.VMEM((SPLIT, rows, cut), BF16),
    ]
    sems = [(5,), (3, 2, NZ), (3, NZ), (3,), (3, NZ), (NX - 1,), (NX - 1,), (2, NX - 1), (2, NX - 1)]
    sems += [(1,), (1,), (2, NY - 1), (2, NY - 1), (1,), (1,)]
    sems += [(NY - 1, 2 * SPLIT), (NY - 1, 2 * SPLIT), (SPLIT,), (SPLIT,)]
    hbm, vmem = pl.BlockSpec(memory_space=pl.ANY), pl.BlockSpec(memory_space=pltpu.VMEM)
    return pl.pallas_call(
        kernel,
        out_shape=jax.ShapeDtypeStruct((rows, width), BF16),
        in_specs=[hbm] * 5,
        out_specs=vmem,
        scratch_shapes=scratch + [dma(s) for s in sems],
        compiler_params=pltpu.CompilerParams(
            collective_id=0, has_side_effects=True, vmem_limit_bytes=60 * 1024 * 1024
        ),
        cost_estimate=pl.CostEstimate(flops=2300000000, bytes_accessed=20000000, transcendentals=0),
    )(tokens, norm_gain.reshape(1, features), w_qkv, conv_filter, w_out)


def solution(mesh):
    placed = (P("seq", "mp"), P(), P(None, "seq", "mp"), P("mp", None), P("mp", None))
    return jax.shard_map(
        local, mesh=mesh, in_specs=placed, out_specs=P("seq", "mp"), check_vma=False
    )
```
